128 devices in a mesh: dap: 32 (over z_lo, y, x), rep: 4 (over z_hi, core).
Axes of the slice: x: 4, y: 4, z: 4 (z_hi: 2, z_lo: 2; z = z_hi * 2 + z_lo), core: 2. Of those that a mesh axis runs over, the one named last changes fastest.
Arguments:
- pair_state: bfloat16 [512, 512, 128], P(('dap', 'rep')), may hold values from -6 to 6
- input_weights: bfloat16 [2, 128, 512], replicated, may hold values from -0.5 to 0.5
- gate_weights: bfloat16 [2, 128, 128], replicated, may hold values from -0.5 to 0.5
- output_weights: bfloat16 [2, 128, 128], replicated, may hold values from -0.5 to 0.5
- input_gains: float32 [2, 128], replicated, may hold values from 0.25 to 1.75
- hidden_gains: float32 [2, 128], replicated, may hold values from 0.25 to 1.75
Outputs:
- updated: bfloat16 [512, 512, 128], P(None, ('dap', 'rep'))
The draws below stay inside these ranges and needn't reach their ends.
All inputs are finite; a program needn't handle non-finite values.
Results may differ from the reference program's by a relative error of at most 0.012.
Values may be sent and summed in bfloat16 or wider, within the bound.
No kernel may reach another device: no remote copies, remote signals or barrier semaphores. Data moves between devices by JAX's collectives and lax.ppermute only.
A program may use at most 64 MiB of HBM per device.

```python
import jax
import jax.numpy as jnp
from jax import lax

CP = 128
CH = 128
ROWS_DEV = 4
TOKENS = 512


def level_of(rng, dims, shards, least, top_value):
    loudness = 1.0
    for dim, parts in shards:
        steps = jax.random.uniform(jax.random.fold_in(jax.random.fold_in(rng, 6), dim), (parts,), jnp.float32, least / len(shards), top_value / len(shards))
        loudness = loudness * jnp.repeat(jnp.exp(steps), dims[dim] // parts).reshape((-1,) + (1,) * (len(dims) - 1 - dim))
    return loudness


def noise(key, shape, width, reach, cuts=(), dtype=jnp.bfloat16):
    level = level_of(key, shape, cuts, -0.22, 0.18) if cuts else 1.0
    values = jax.random.normal(key, shape, jnp.float32) * width * level
    return jnp.minimum(jnp.maximum(values, -reach), reach).astype(dtype)


def setup_inputs(seed: int = 0) -> dict:
    splits = jax.random.split(jax.random.key(seed), 7)
    return {
        "pair_state": noise(splits[0], (TOKENS, TOKENS, CP), 1.0, 6.0, ((0, 128),)),
        "input_weights": noise(splits[1], (2, CP, 4 * CH), CP ** -0.5, 0.5),
        "gate_weights": noise(splits[2], (2, CP, CP), CP ** -0.5, 0.5),
        "output_weights": noise(splits[3], (2, CH, CP), CH ** -0.5, 0.5),
        "input_gains": jnp.clip(1.0 + 0.15 * jax.random.normal(splits[4], (2, CP), jnp.float32), 0.25, 1.75),
        "hidden_gains": jnp.clip(1.0 + 0.15 * jax.random.normal(splits[5], (2, CH), jnp.float32), 0.25, 1.75),
    }


epsilon = 1e-05

def layer_norm(values, scales):
    average = lax.optimization_barrier(jnp.mean(values, axis=-1, keepdims=True))
    centred = values - average
    variance = lax.optimization_barrier(jnp.mean(centred * centred, axis=-1, keepdims=True))
    return centred * lax.rsqrt(variance + epsilon) * scales

def prepare_rows(row_block, weights, scales):
    normed = layer_norm(row_block.astype(jnp.float32), scales).astype(jnp.bfloat16)
    flattened = normed.reshape(-1, CP)
    outputs = []
    for half_index in range(2):
        linear = jnp.dot(flattened, weights[:, 2 * half_index * CH:(2 * half_index + 1) * CH], preferred_element_type=jnp.float32)
        gating = jnp.dot(flattened, weights[:, (2 * half_index + 1) * CH:(2 * half_index + 2) * CH], preferred_element_type=jnp.float32)
        product = (jax.nn.sigmoid(gating) * linear).astype(jnp.bfloat16)
        outputs.append(product.reshape(row_block.shape[0], TOKENS, CH))
    return (outputs[0], outputs[1])

def mix_groups(operands):
    left_group, right_group = operands
    mixed = jnp.einsum('gik,gjk->gij', left_group.astype(jnp.float32), right_group.astype(jnp.float32))
    return mixed.astype(jnp.bfloat16)

def finish_rows(operands, gate_matrix, output_matrix, input_scales, hidden_scales):
    row_block, mixed_block = operands
    normed = layer_norm(row_block.astype(jnp.float32), input_scales).astype(jnp.bfloat16)
    gating = jax.nn.sigmoid(jnp.dot(normed.reshape(-1, CP), gate_matrix, preferred_element_type=jnp.float32))
    hidden = layer_norm(mixed_block.astype(jnp.float32), hidden_scales).astype(jnp.bfloat16)
    update_term = jnp.dot(hidden.reshape(-1, CH), output_matrix, preferred_element_type=jnp.float32)
    total = row_block.astype(jnp.float32).reshape(-1, CP) + gating * update_term
    return total.astype(jnp.bfloat16).reshape(row_block.shape)

def apply_update(state, layer_index, incoming, input_weights, gate_weights, output_weights, input_gains, hidden_gains):
    block_count = TOKENS // ROWS_DEV
    blocks = state.reshape(block_count, ROWS_DEV, TOKENS, CP)
    left_side, right_side = lax.map(lambda row_block: prepare_rows(row_block, input_weights[layer_index], input_gains[layer_index]), blocks)
    left_side = left_side.reshape(TOKENS, TOKENS, CH)
    right_side = right_side.reshape(TOKENS, TOKENS, CH)
    if incoming:
        left_side = jnp.swapaxes(left_side, 0, 1)
        right_side = jnp.swapaxes(right_side, 0, 1)
    left_groups = jnp.moveaxis(left_side, 2, 0).reshape(CH // 8, 8, TOKENS, TOKENS)
    right_groups = jnp.moveaxis(right_side, 2, 0).reshape(CH // 8, 8, TOKENS, TOKENS)
    mixed = lax.map(mix_groups, (left_groups, right_groups)).reshape(CH, TOKENS, TOKENS)
    mixed = jnp.moveaxis(mixed, 0, 2).reshape(block_count, ROWS_DEV, TOKENS, CH)
    finished = lax.map(lambda operands: finish_rows(operands, gate_weights[layer_index], output_weights[layer_index], input_gains[layer_index], hidden_gains[layer_index]), (blocks, mixed))
    return finished.reshape(TOKENS, TOKENS, CP)

def reference(pair_state, input_weights, gate_weights, output_weights, input_gains, hidden_gains):
    middle = apply_update(pair_state, 0, False, input_weights, gate_weights, output_weights, input_gains, hidden_gains)
    return apply_update(middle, 1, True, input_weights, gate_weights, output_weights, input_gains, hidden_gains)
```

```python
import functools

import jax
import jax.numpy as jnp
from jax import lax
from jax.experimental import pallas as pl
from jax.experimental.pallas import tpu as pltpu
from jax.sharding import PartitionSpec as P

epsilon = 1e-05
AXES = ("dap", "rep")
F32 = jnp.float32
BF16 = jnp.bfloat16
LANES = 128
VMEM_LIMIT = 40 * 1024 * 1024


def dot_nn(a, b):
    return lax.dot_general(a, b, (((1,), (0,)), ((), ())), preferred_element_type=F32)


def dot_nt(a, b):
    return lax.dot_general(a, b, (((1,), (1,)), ((), ())), preferred_element_type=F32)


def half_sigmoid(x):
    return 0.5 * jnp.tanh(x) + 0.5


def norm_lanes(x, x16, ones, gain):
    cen = x - dot_nn(x16, ones)
    sq = cen * cen
    high = sq.astype(BF16)
    low = (sq - high.astype(F32)).astype(BF16)
    var = dot_nn(high, ones) + dot_nn(low, ones)
    return (cen * lax.rsqrt(var + epsilon) * gain).astype(BF16)


def norm_rows(x, gain):
    cen = x - jnp.mean(x, axis=0, keepdims=True)
    var = jnp.mean(cen * cen, axis=0, keepdims=True)
    return (cen * lax.rsqrt(var + epsilon) * gain).astype(BF16)


def store_operands(pt, index, left_s, right_s):
    ch = pt.shape[0] // 4
    chunks = pt.shape[1] // LANES
    left = half_sigmoid(pt[ch : 2 * ch]) * pt[:ch]
    right = half_sigmoid(pt[3 * ch :]) * pt[2 * ch : 3 * ch]
    for c in range(chunks):
        sl = pl.ds(index * chunks + c, ch, stride=16)
        left_s[sl, :] = left[:, c * LANES : (c + 1) * LANES]
        right_s[sl, :] = right[:, c * LANES : (c + 1) * LANES]


def prepare_kernel(x_ref, wt_ref, gain_ref, ones_ref, out_ref, left_s, right_s, state_s, x_s):
    rows, tokens, _ = x_ref.shape
    peers = out_ref.shape[0]
    cols = tokens // peers
    for i in range(rows):
        x16 = x_ref[i]
        x = x16.astype(F32)
        x_s[...] = x
        normed = norm_lanes(x, x16, ones_ref[...], gain_ref[...])
        store_operands(dot_nt(wt_ref[...], normed), i, left_s, right_s)
        for j in range(cols):
            state_s[pl.ds(i * cols + j, peers, stride=16), :] = x_s[pl.ds(j, peers, stride=cols), :]
    for part, ref in enumerate((left_s, right_s, state_s)):
        out_ref[:, 16 * part : 16 * (part + 1), :] = ref[...].reshape(peers, 16, LANES).astype(BF16)


def mix_kernel(in_ref, out_ref, left_s, right_s, left_b, right_b):
    peers = in_ref.shape[0]
    tokens = left_b.shape[0]
    chunks = tokens // LANES
    for part, (wide, whole) in enumerate(((left_s, left_b), (right_s, right_b))):
        wide[...] = in_ref[:, 16 * part : 16 * (part + 1), :].astype(F32).reshape(peers * 16, LANES)
        for c in range(chunks):
            whole[:, c * LANES : (c + 1) * LANES] = wide[pl.ds(c, tokens, stride=chunks), :].astype(BF16)
    for c in range(chunks):
        left_s[pl.ds(c, tokens, stride=chunks), :] = dot_nt(
            right_b[...], left_b[c * LANES : (c + 1) * LANES, :]
        )
    out_ref[...] = left_s[...].reshape(peers, 16, LANES).astype(BF16)


def gate_first_kernel(in_ref, gt_ref, gain_ref, ones_ref, state_ref, gate_ref, wide):
    peers = in_ref.shape[0]
    cols, _, tokens = state_ref.shape
    wide[...] = in_ref[:, 32:48, :].astype(F32).reshape(peers * 16, LANES)
    for j in range(cols):
        x = wide[pl.ds(j, tokens, stride=cols), :]
        normed = norm_lanes(x, x.astype(BF16), ones_ref[...], gain_ref[...])
        gate_ref[j] = half_sigmoid(dot_nt(gt_ref[...], normed))
        state_ref[j] = x.T.astype(BF16)


def gate_second_kernel(state_ref, gt_ref, gain_ref, gate_ref):
    for j in range(state_ref.shape[0]):
        normed = norm_rows(state_ref[j].astype(F32), gain_ref[...])
        gate_ref[j] = half_sigmoid(dot_nn(gt_ref[...], normed))


def normalize_mixed(mixed_ref, wide):
    y = mixed_ref[...].astype(F32)
    cen = y - jnp.mean(y, axis=0, keepdims=True)
    var = jnp.mean(cen * cen, axis=0, keepdims=True)
    wide[...] = (cen * lax.rsqrt(var + epsilon)).reshape(wide.shape)


def hidden_of(wide, j, chunks, gain):
    channels = gain.shape[0]
    return jnp.concatenate(
        [
            (wide[pl.ds(j * chunks + c, channels, stride=16), :] * gain).astype(BF16)
            for c in range(chunks)
        ],
        axis=1,
    )


def middle_kernel(
    mixed_ref, state_ref, gate_ref, hgain_ref, ot_ref, igain_ref, wt_ref, out_ref, next_ref, wide, left_s, right_s
):
    cols, _, tokens = state_ref.shape
    chunks = tokens // LANES
    peers = out_ref.shape[0]
    normalize_mixed(mixed_ref, wide)
    for j in range(cols):
        update = dot_nn(ot_ref[...], hidden_of(wide, j, chunks, hgain_ref[...]))
        state = (state_ref[j].astype(F32) + gate_ref[j] * update).astype(BF16)
        next_ref[j] = state
        normed = norm_rows(state.astype(F32), igain_ref[...])
        store_operands(dot_nn(wt_ref[...], normed), j, left_s, right_s)
    for part, ref in enumerate((left_s, right_s)):
        out_ref[:, 16 * part : 16 * (part + 1), :] = ref[...].reshape(peers, 16, LANES).astype(BF16)


def last_kernel(mixed_ref, state_ref, gate_ref, hgain_ref, ot_ref, out_ref, wide, out_s):
    cols, _, tokens = state_ref.shape
    chunks = tokens // LANES
    normalize_mixed(mixed_ref, wide)
    for j in range(cols):
        update = dot_nn(ot_ref[...], hidden_of(wide, j, chunks, hgain_ref[...]))
        state = state_ref[j].astype(F32) + gate_ref[j] * update
        out_s[pl.ds(j, tokens, stride=cols), :] = state.T
    out_ref[...] = out_s[...].astype(BF16)


def call(kernel, out_shape, scratch, flops, moved, *args):
    return pl.pallas_call(
        kernel,
        out_shape=out_shape,
        scratch_shapes=[pltpu.VMEM(shape, dtype) for shape, dtype in scratch],
        compiler_params=pltpu.CompilerParams(vmem_limit_bytes=VMEM_LIMIT),
        cost_estimate=pl.CostEstimate(flops=flops, bytes_accessed=moved, transcendentals=0),
    )(*args)


def exchange(buffer):
    return lax.all_to_all(buffer, AXES, split_axis=0, concat_axis=0, tiled=True)


def on_device(pair_state, input_weights, gate_weights, output_weights, input_gains, hidden_gains):
    rows, tokens, cp = pair_state.shape
    ch = output_weights.shape[1]
    peers = tokens // rows
    shape = jax.ShapeDtypeStruct
    positions = rows * tokens
    wide = ((positions, LANES), F32)
    whole = ((tokens, tokens), BF16)
    size = positions * ch * 2

    halves = jnp.repeat(jnp.array([1.0, 0.5, 1.0, 0.5], BF16), ch)[None, :, None]
    wt = jnp.swapaxes(input_weights, 1, 2) * halves
    gt = jnp.swapaxes(gate_weights, 1, 2) * jnp.array(0.5, BF16)
    ot = jnp.swapaxes(output_weights, 1, 2)
    gain_wide = input_gains[1][:, None]
    hidden_wide = hidden_gains[:, :, None]
    ones = jnp.full((cp, cp), 1.0 / cp, BF16)
    project = 2 * positions * cp * 4 * ch
    mixing = 2 * tokens**3
    small = 2 * positions * cp * ch

    sent = call(
        prepare_kernel,
        shape((peers, 48, LANES), BF16),
        [wide, wide, wide, ((tokens, cp), F32)],
        project,
        4 * size,
        pair_state,
        wt[0],
        input_gains[:1],
        ones,
    )
    got = exchange(sent)
    mix = functools.partial(
        call,
        mix_kernel,
        shape((peers, 16, LANES), BF16),
        [wide, wide, whole, whole],
        mixing,
        3 * size,
    )
    mixed = exchange(mix(got))
    transposed = shape((rows, cp, tokens), BF16)
    gating = shape((rows, cp, tokens), F32)
    state, gate = call(
        gate_first_kernel,
        (transposed, gating),
        [wide],
        2 * small,
        5 * size,
        got,
        gt[0],
        input_gains[:1],
        ones,
    )
    sent, state = call(
        middle_kernel,
        (shape((peers, 32, LANES), BF16), transposed),
        [wide, wide, wide],
        project + small,
        6 * size,
        mixed,
        state,
        gate,
        hidden_wide[0],
        ot[0],
        gain_wide,
        wt[1],
    )
    mixed = exchange(mix(exchange(sent)))
    gate = call(gate_second_kernel, gating, [], small, 3 * size, state, gt[1], gain_wide)
    out = call(
        last_kernel,
        shape((positions, cp), BF16),
        [wide, wide],
        small,
        5 * size,
        mixed,
        state,
        gate,
        hidden_wide[1],
        ot[1],
    )
    return out.reshape(tokens, rows, cp)


def solution(mesh):
    return jax.shard_map(
        on_device,
        mesh=mesh,
        in_specs=(P(AXES, None, None), P(), P(), P(), P(), P()),
        out_specs=P(None, AXES, None),
        check_vma=False,
    )
```

```python
import functools

import jax
import jax.numpy as jnp
from jax import lax
from jax.experimental import pallas as pl
from jax.experimental.pallas import tpu as pltpu
from jax.sharding import PartitionSpec as P

epsilon = 1e-05
AXES = ("dap", "rep")
F32 = jnp.float32
BF16 = jnp.bfloat16
LANES = 128
VMEM_LIMIT = 24 * 1024 * 1024


def dot_nn(a, b):
    return lax.dot_general(a, b, (((1,), (0,)), ((), ())), preferred_element_type=F32)


def dot_nt(a, b):
    return lax.dot_general(a, b, (((1,), (1,)), ((), ())), preferred_element_type=F32)


def half_sigmoid(x):
    return 0.5 * jnp.tanh(x) + 0.5


def norm_lanes(x, gain):
    cen = x - jnp.mean(x, axis=1, keepdims=True)
    var = jnp.mean(cen * cen, axis=1, keepdims=True)
    return (cen * lax.rsqrt(var + epsilon) * gain).astype(BF16)


def norm_wide(x, gain_ref):
    cen = x - jnp.mean(x, axis=0, keepdims=True)
    var = jnp.mean(cen * cen, axis=0, keepdims=True)
    unit = cen * lax.rsqrt(var + epsilon)
    return jnp.concatenate(
        [
            (unit[:, c : c + LANES] * gain_ref[...]).astype(BF16)
            for c in range(0, x.shape[1], LANES)
        ],
        axis=1,
    )


def store_operands(pt, index, left_s, right_s):
    ch = pt.shape[0] // 4
    chunks = pt.shape[1] // LANES
    left = half_sigmoid(pt[ch : 2 * ch]) * pt[:ch]
    right = half_sigmoid(pt[3 * ch :]) * pt[2 * ch : 3 * ch]
    for c in range(chunks):
        sl = pl.ds(index * chunks + c, ch, stride=16)
        left_s[sl, :] = left[:, c * LANES : (c + 1) * LANES]
        right_s[sl, :] = right[:, c * LANES : (c + 1) * LANES]


def flip(block, factor=1.0):
    return (block.astype(F32).T * factor).astype(BF16)


def flip_projections(w_ref, update, wt_ref):
    ch = w_ref.shape[2] // 4
    for part in range(4):
        block = w_ref[update, :, part * ch : (part + 1) * ch]
        wt_ref[part * ch : (part + 1) * ch, :] = flip(block, 0.5 if part % 2 else 1.0)


def widen(gain):
    return jnp.broadcast_to(gain, (LANES, gain.shape[1])).T


def prepare_kernel(x_ref, w_ref, gain_ref, out_ref, wt_s, left_s, right_s, state_s, x_s):
    rows, tokens, _ = x_ref.shape
    peers = out_ref.shape[0]
    cols = tokens // peers
    flip_projections(w_ref, 0, wt_s)
    for i in range(rows):
        x = x_ref[i].astype(F32)
        x_s[...] = x
        store_operands(dot_nt(wt_s[...], norm_lanes(x, gain_ref[0:1, :])), i, left_s, right_s)
        for j in range(cols):
            state_s[pl.ds(i * cols + j, peers, stride=16), :] = x_s[pl.ds(j, peers, stride=cols), :]
    for part, ref in enumerate((left_s, right_s, state_s)):
        out_ref[:, 16 * part : 16 * (part + 1), :] = ref[...].reshape(peers, 16, LANES).astype(BF16)


def mix_kernel(in_ref, out_ref, left_s, right_s, left_b, right_b):
    peers = in_ref.shape[0]
    tokens = left_b.shape[0]
    chunks = tokens // LANES
    for part, (wide, whole) in enumerate(((left_s, left_b), (right_s, right_b))):
        wide[...] = in_ref[:, 16 * part : 16 * (part + 1), :].astype(F32).reshape(peers * 16, LANES)
        for c in range(chunks):
            whole[:, c * LANES : (c + 1) * LANES] = wide[pl.ds(c, tokens, stride=chunks), :].astype(BF16)
    mixed = dot_nt(right_b[...], left_b[...])
    for c in range(chunks):
        left_s[pl.ds(c, tokens, stride=chunks), :] = mixed[:, c * LANES : (c + 1) * LANES]
    out_ref[...] = left_s[...].reshape(peers, 16, LANES).astype(BF16)


def gate_first_kernel(
    in_ref, w_ref, g_ref, o_ref, igain_ref, hgain_ref, state_ref, gate_ref, wt_ref, gt_ref, ot_ref, iwide_ref, hwide_ref, wide
):
    peers = in_ref.shape[0]
    cols, _, tokens = state_ref.shape
    wide[...] = in_ref[:, 32:48, :].astype(F32).reshape(peers * 16, LANES)
    first = flip(g_ref[0], 0.5)
    for j in range(cols):
        x = wide[pl.ds(j, tokens, stride=cols), :]
        normed = norm_lanes(x, igain_ref[0:1, :])
        gate_ref[j] = half_sigmoid(dot_nt(first, normed))
        state_ref[j] = x.T.astype(BF16)
    flip_projections(w_ref, 1, wt_ref)
    gt_ref[...] = flip(g_ref[1], 0.5)
    iwide_ref[...] = widen(igain_ref[1:2, :])
    for update in range(2):
        ot_ref[update] = flip(o_ref[update])
        hwide_ref[update] = widen(hgain_ref[update : update + 1, :])


def gate_second_kernel(state_ref, gt_ref, igain_ref, gate_ref):
    for j in range(state_ref.shape[0]):
        normed = norm_wide(state_ref[j].astype(F32), igain_ref)
        gate_ref[j] = half_sigmoid(dot_nn(gt_ref[...], normed))


def normalize_mixed(mixed_ref, wide):
    y = mixed_ref[...].astype(F32)
    cen = y - jnp.mean(y, axis=0, keepdims=True)
    var = jnp.mean(cen * cen, axis=0, keepdims=True)
    wide[...] = (cen * lax.rsqrt(var + epsilon)).reshape(wide.shape)


def hidden_of(wide, update, j, chunks, gain_ref):
    channels = gain_ref.shape[1]
    return jnp.concatenate(
        [
            (wide[pl.ds(j * chunks + c, channels, stride=16), :] * gain_ref[update]).astype(BF16)
            for c in range(chunks)
        ],
        axis=1,
    )


def middle_kernel(
    mixed_ref, state_ref, gate_ref, hgain_ref, ot_ref, igain_ref, wt_ref, out_ref, next_ref, wide, left_s, right_s
):
    cols, _, tokens = state_ref.shape
    chunks = tokens // LANES
    peers = out_ref.shape[0]
    normalize_mixed(mixed_ref, wide)
    for j in range(cols):
        update = dot_nn(ot_ref[0], hidden_of(wide, 0, j, chunks, hgain_ref))
        state = (state_ref[j].astype(F32) + gate_ref[j] * update).astype(BF16)
        next_ref[j] = state
        normed = norm_wide(state.astype(F32), igain_ref)
        store_operands(dot_nn(wt_ref[...], normed), j, left_s, right_s)
    for part, ref in enumerate((left_s, right_s)):
        out_ref[:, 16 * part : 16 * (part + 1), :] = ref[...].reshape(peers, 16, LANES).astype(BF16)


def last_kernel(mixed_ref, state_ref, gate_ref, hgain_ref, ot_ref, out_ref, wide, out_s):
    cols, _, tokens = state_ref.shape
    chunks = tokens // LANES
    normalize_mixed(mixed_ref, wide)
    for j in range(cols):
        update = dot_nn(ot_ref[1], hidden_of(wide, 1, j, chunks, hgain_ref))
        state = (state_ref[j].astype(F32) + gate_ref[j] * update).astype(BF16)
        out_s[pl.ds(j, tokens, stride=cols), :] = state.T.astype(F32)
    out_ref[...] = out_s[...].astype(BF16)


def call(kernel, out_shape, scratch, flops, moved, *args):
    return pl.pallas_call(
        kernel,
        out_shape=out_shape,
        scratch_shapes=[pltpu.VMEM(shape, dtype) for shape, dtype in scratch],
        compiler_params=pltpu.CompilerParams(vmem_limit_bytes=VMEM_LIMIT),
        cost_estimate=pl.CostEstimate(flops=flops, bytes_accessed=moved, transcendentals=0),
        name=kernel.__name__,
    )(*args)


def exchange(buffer):
    return lax.all_to_all(buffer, AXES, split_axis=0, concat_axis=0, tiled=True)


def on_device(pair_state, input_weights, gate_weights, output_weights, input_gains, hidden_gains):
    rows, tokens, cp = pair_state.shape
    ch = output_weights.shape[1]
    peers = tokens // rows
    shape = jax.ShapeDtypeStruct
    positions = rows * tokens
    wide = ((positions, LANES), F32)
    whole = ((tokens, tokens), BF16)
    size = positions * ch * 2
    project = 2 * positions * cp * 4 * ch
    small = 2 * positions * cp * ch
    mix = functools.partial(
        call,
        mix_kernel,
        shape((peers, 16, LANES), BF16),
        [wide, wide, whole, whole],
        2 * tokens**3,
        3 * size,
    )
    transposed = shape((rows, cp, tokens), BF16)
    gating = shape((rows, cp, tokens), F32)

    sent = call(
        prepare_kernel,
        shape((peers, 48, LANES), BF16),
        [((4 * ch, cp), BF16), wide, wide, wide, ((tokens, cp), F32)],
        project,
        4 * size,
        pair_state,
        input_weights,
        input_gains,
    )
    got = exchange(sent)
    mixed = exchange(mix(got))
    state, gate, wt, gt, ot, iwide, hwide = call(
        gate_first_kernel,
        (
            transposed,
            gating,
            shape((4 * ch, cp), BF16),
            shape((cp, cp), BF16),
            shape((2, cp, ch), BF16),
            shape((cp, LANES), F32),
            shape((2, ch, LANES), F32),
        ),
        [wide],
        2 * small,
        5 * size,
        got,
        input_weights,
        gate_weights,
        output_weights,
        input_gains,
        hidden_gains,
    )
    sent, state = call(
        middle_kernel,
        (shape((peers, 32, LANES), BF16), transposed),
        [wide, wide, wide],
        project + small,
        6 * size,
        mixed,
        state,
        gate,
        hwide,
        ot,
        iwide,
        wt,
    )
    mixed = exchange(mix(exchange(sent)))
    gate = call(gate_second_kernel, gating, [], small, 3 * size, state, gt, iwide)
    out = call(
        last_kernel,
        shape((positions, cp), BF16),
        [wide, wide],
        small,
        5 * size,
        mixed,
        state,
        gate,
        hwide,
        ot,
    )
    return out.reshape(tokens, rows, cp)


def solution(mesh):
    return jax.shard_map(
        on_device,
        mesh=mesh,
        in_specs=(P(AXES, None, None), P(), P(), P(), P(), P()),
        out_specs=P(None, AXES, None),
        check_vma=False,
    )
```

```python
import functools

import jax
import jax.numpy as jnp
from jax import lax
from jax.experimental import pallas as pl
from jax.experimental.pallas import tpu as pltpu
from jax.sharding import PartitionSpec as P

epsilon = 1e-05
AXES = ("dap", "rep")
F32 = jnp.float32
BF16 = jnp.bfloat16
LANES = 128
VMEM_LIMIT = 24 * 1024 * 1024
VMEM_SIZE = 64 * 1024 * 1024


def dot_nn(a, b):
    return lax.dot_general(a, b, (((1,), (0,)), ((), ())), preferred_element_type=F32)


def dot_nt(a, b):
    return lax.dot_general(a, b, (((1,), (1,)), ((), ())), preferred_element_type=F32)


def half_sigmoid(x):
    return 0.5 * jnp.tanh(x) + 0.5


def norm_lanes(x, gain):
    cen = x - jnp.mean(x, axis=1, keepdims=True)
    var = jnp.mean(cen * cen, axis=1, keepdims=True)
    return (cen * lax.rsqrt(var + epsilon) * gain).astype(BF16)


def norm_wide(x, gain_ref):
    cen = x - jnp.mean(x, axis=0, keepdims=True)
    var = jnp.mean(cen * cen, axis=0, keepdims=True)
    unit = cen * lax.rsqrt(var + epsilon)
    return jnp.concatenate(
        [
            (unit[:, c : c + LANES] * gain_ref[...]).astype(BF16)
            for c in range(0, x.shape[1], LANES)
        ],
        axis=1,
    )


def store_operands(pt, index, left_s, right_s):
    ch = pt.shape[0] // 4
    chunks = pt.shape[1] // LANES
    left = half_sigmoid(pt[ch : 2 * ch]) * pt[:ch]
    right = half_sigmoid(pt[3 * ch :]) * pt[2 * ch : 3 * ch]
    for c in range(chunks):
        sl = pl.ds(index * chunks + c, ch, stride=16)
        left_s[sl, :] = left[:, c * LANES : (c + 1) * LANES]
        right_s[sl, :] = right[:, c * LANES : (c + 1) * LANES]


def send_out(parts, out_s, out_hbm, out_sem):
    pieces = out_sem.shape[0]
    size = out_s.shape[0] // pieces
    copies = []
    for p in range(pieces):
        peers = slice(p * size, (p + 1) * size)
        for part, ref in enumerate(parts):
            block = ref[p * size * 16 : (p + 1) * size * 16, :]
            out_s[peers, 16 * part : 16 * (part + 1), :] = block.reshape(size, 16, LANES).astype(BF16)
        copies.append(pltpu.make_async_copy(out_s.at[peers], out_hbm.at[peers], out_sem.at[p]))
        copies[-1].start()
    for copy in copies:
        copy.wait()


def flip(block, factor=1.0):
    return (block.astype(F32).T * factor).astype(BF16)


def flip_projections(w_ref, update, wt_ref):
    ch = w_ref.shape[2] // 4
    for part in range(4):
        block = w_ref[update, :, part * ch : (part + 1) * ch]
        wt_ref[part * ch : (part + 1) * ch, :] = flip(block, 0.5 if part % 2 else 1.0)


def widen(gain):
    return jnp.broadcast_to(gain, (LANES, gain.shape[1])).T


def prepare_kernel(
    x_hbm, w_hbm, gain_hbm, out_hbm, x_ref, w_ref, gain_ref, wt_s, left_s, right_s, state_s, x_s, out_s, x_sem, w_sem, gain_sem, out_sem
):
    rows, tokens, _ = x_ref.shape
    peers = out_s.shape[0]
    cols = tokens // peers
    w_copy = pltpu.make_async_copy(w_hbm.at[0:1], w_ref, w_sem)
    gain_copy = pltpu.make_async_copy(gain_hbm, gain_ref, gain_sem)
    x_copies = [pltpu.make_async_copy(x_hbm.at[i], x_ref.at[i], x_sem.at[i]) for i in range(rows)]
    w_copy.start()
    gain_copy.start()
    for copy in x_copies:
        copy.start()
    w_copy.wait()
    flip_projections(w_ref, 0, wt_s)
    gain_copy.wait()
    for i in range(rows):
        x_copies[i].wait()
        x = x_ref[i].astype(F32)
        x_s[...] = x
        store_operands(dot_nt(wt_s[...], norm_lanes(x, gain_ref[0:1, :])), i, left_s, right_s)
        for j in range(cols):
            state_s[pl.ds(i * cols + j, peers, stride=16), :] = x_s[pl.ds(j, peers, stride=cols), :]
    send_out((left_s, right_s, state_s), out_s, out_hbm, out_sem)


def mix_first_kernel(in_ref, out_hbm, state_ref, *scratch):
    state_ref[...] = in_ref[:, 32:48, :]
    mix_kernel(in_ref, out_hbm, *scratch)


def mix_kernel(in_ref, out_hbm, left_s, right_s, left_b, right_b, out_s, out_sem):
    peers = in_ref.shape[0]
    tokens = left_b.shape[0]
    chunks = tokens // LANES
    for part, (wide, whole) in enumerate(((left_s, left_b), (right_s, right_b))):
        wide[...] = in_ref[:, 16 * part : 16 * (part + 1), :].astype(F32).reshape(peers * 16, LANES)
        for c in range(chunks):
            whole[:, c * LANES : (c + 1) * LANES] = wide[pl.ds(c, tokens, stride=chunks), :].astype(BF16)
    mixed = dot_nt(right_b[...], left_b[...])
    for c in range(chunks):
        left_s[pl.ds(c, tokens, stride=chunks), :] = mixed[:, c * LANES : (c + 1) * LANES]
    send_out((left_s,), out_s, out_hbm, out_sem)


def gate_first_kernel(
    in_ref, w_ref, g_ref, o_ref, igain_ref, hgain_ref, state_ref, gate_ref, wt_ref, gt_ref, ot_ref, iwide_ref, hwide_ref, wide
):
    peers = in_ref.shape[0]
    cols, _, tokens = state_ref.shape
    wide[...] = in_ref[...].astype(F32).reshape(peers * 16, LANES)
    first = flip(g_ref[0], 0.5)
    for j in range(cols):
        x = wide[pl.ds(j, tokens, stride=cols), :]
        normed = norm_lanes(x, igain_ref[0:1, :])
        gate_ref[j] = half_sigmoid(dot_nt(first, normed))
        state_ref[j] = x.T.astype(BF16)
    flip_projections(w_ref, 1, wt_ref)
    gt_ref[...] = flip(g_ref[1], 0.5)
    iwide_ref[...] = widen(igain_ref[1:2, :])
    for update in range(2):
        ot_ref[update] = flip(o_ref[update])
        hwide_ref[update] = widen(hgain_ref[update : update + 1, :])


def gate_second_kernel(state_ref, gt_ref, igain_ref, gate_ref):
    for j in range(state_ref.shape[0]):
        normed = norm_wide(state_ref[j].astype(F32), igain_ref)
        gate_ref[j] = half_sigmoid(dot_nn(gt_ref[...], normed))


def normalize_mixed(mixed_ref, wide):
    y = mixed_ref[...].astype(F32)
    cen = y - jnp.mean(y, axis=0, keepdims=True)
    var = jnp.mean(cen * cen, axis=0, keepdims=True)
    wide[...] = (cen * lax.rsqrt(var + epsilon)).reshape(wide.shape)


def hidden_of(wide, update, j, chunks, gain_ref):
    channels = gain_ref.shape[1]
    return jnp.concatenate(
        [
            (wide[pl.ds(j * chunks + c, channels, stride=16), :] * gain_ref[update]).astype(BF16)
            for c in range(chunks)
        ],
        axis=1,
    )


def middle_kernel(
    mixed_ref, state_ref, gate_ref, hgain_ref, ot_ref, igain_ref, wt_ref, out_ref, next_ref, wide, left_s, right_s
):
    cols, _, tokens = state_ref.shape
    chunks = tokens // LANES
    peers = out_ref.shape[0]
    normalize_mixed(mixed_ref, wide)
    for j in range(cols):
        update = dot_nn(ot_ref[0], hidden_of(wide, 0, j, chunks, hgain_ref))
        state = (state_ref[j].astype(F32) + gate_ref[j] * update).astype(BF16)
        next_ref[j] = state
        normed = norm_wide(state.astype(F32), igain_ref)
        store_operands(dot_nn(wt_ref[...], normed), j, left_s, right_s)
    for part, ref in enumerate((left_s, right_s)):
        out_ref[:, 16 * part : 16 * (part + 1), :] = ref[...].reshape(peers, 16, LANES).astype(BF16)


def last_kernel(mixed_ref, state_ref, gate_ref, hgain_ref, ot_ref, out_ref, wide, out_s):
    cols, _, tokens = state_ref.shape
    chunks = tokens // LANES
    normalize_mixed(mixed_ref, wide)
    for j in range(cols):
        update = dot_nn(ot_ref[1], hidden_of(wide, 1, j, chunks, hgain_ref))
        state = (state_ref[j].astype(F32) + gate_ref[j] * update).astype(BF16)
        out_s[pl.ds(j, tokens, stride=cols), :] = state.T.astype(F32)
    out_ref[...] = out_s[...].astype(BF16)


def call(kernel, out_shape, scratch, flops, moved, args, limit=VMEM_LIMIT, **options):
    return pl.pallas_call(
        kernel,
        out_shape=out_shape,
        scratch_shapes=[pltpu.VMEM(*spec) if isinstance(spec, tuple) else spec for spec in scratch],
        compiler_params=pltpu.CompilerParams(vmem_limit_bytes=limit),
        cost_estimate=pl.CostEstimate(flops=flops, bytes_accessed=moved, transcendentals=0),
        name=kernel.__name__,
        **options,
    )(*args)


def exchange(buffer):
    return lax.all_to_all(buffer, AXES, split_axis=0, concat_axis=0, tiled=True)


def on_device(pair_state, input_weights, gate_weights, output_weights, input_gains, hidden_gains):
    rows, tokens, cp = pair_state.shape
    ch = output_weights.shape[1]
    peers = tokens // rows
    shape = jax.ShapeDtypeStruct
    positions = rows * tokens
    wide = ((positions, LANES), F32)
    whole = ((tokens, tokens), BF16)
    size = positions * ch * 2
    project = 2 * positions * cp * 4 * ch
    small = 2 * positions * cp * ch
    packed = shape((peers, 16, LANES), BF16)
    mix = functools.partial(
        call,
        scratch=[wide, wide, whole, whole, ((peers, 16, LANES), BF16), pltpu.SemaphoreType.DMA((4,))],
        flops=2 * tokens**3,
        moved=3 * size,
    )
    transposed = shape((rows, cp, tokens), BF16)
    gating = shape((rows, cp, tokens), F32)

    sent = call(
        prepare_kernel,
        shape((peers, 48, LANES), BF16),
        [
            ((rows, tokens, cp), BF16),
            ((1, cp, 4 * ch), BF16),
            ((2, cp), F32),
            ((4 * ch, cp), BF16),
            wide,
            wide,
            wide,
            ((tokens, cp), F32),
            ((peers, 48, LANES), BF16),
            pltpu.SemaphoreType.DMA((rows,)),
            pltpu.SemaphoreType.DMA,
            pltpu.SemaphoreType.DMA,
            pltpu.SemaphoreType.DMA((4,)),
        ],
        project,
        4 * size,
        args=(pair_state, input_weights, input_gains),
        limit=60 * 1024 * 1024,
        in_specs=[pl.BlockSpec(memory_space=pltpu.HBM)] * 3,
        out_specs=pl.BlockSpec(memory_space=pltpu.HBM),
    )
    in_hbm, in_vmem = (pl.BlockSpec(memory_space=m) for m in (pltpu.HBM, pltpu.VMEM))
    mixed, state = mix(
        mix_first_kernel, (packed, packed), args=(exchange(sent),), out_specs=(in_hbm, in_vmem)
    )
    mixed = exchange(mixed)
    state, gate, wt, gt, ot, iwide, hwide = call(
        gate_first_kernel,
        (
            transposed,
            gating,
            shape((4 * ch, cp), BF16),
            shape((cp, cp), BF16),
            shape((2, cp, ch), BF16),
            shape((cp, LANES), F32),
            shape((2, ch, LANES), F32),
        ),
        [wide],
        2 * small,
        5 * size,
        args=(state, input_weights, gate_weights, output_weights, input_gains, hidden_gains),
    )
    sent, state = call(
        middle_kernel,
        (shape((peers, 32, LANES), BF16), transposed),
        [wide, wide, wide],
        project + small,
        6 * size,
        args=(mixed, state, gate, hwide, ot, iwide, wt),
    )
    mixed = exchange(mix(mix_kernel, packed, args=(exchange(sent),), out_specs=in_hbm))
    gate = call(gate_second_kernel, gating, [], small, 3 * size, (state, gt, iwide))
    out = call(
        last_kernel,
        shape((positions, cp), BF16),
        [wide, wide],
        small,
        5 * size,
        args=(mixed, state, gate, hwide, ot),
    )
    return out.reshape(tokens, rows, cp)


def solution(mesh):
    return jax.shard_map(
        on_device,
        mesh=mesh,
        in_specs=(P(AXES, None, None), P(), P(), P(), P(), P()),
        out_specs=P(None, AXES, None),
        check_vma=False,
    )
```

```python
import functools

import jax
import jax.numpy as jnp
from jax import lax
from jax.experimental import pallas as pl
from jax.experimental.pallas import tpu as pltpu
from jax.sharding import PartitionSpec as P

epsilon = 1e-05
AXES = ("dap", "rep")
F32 = jnp.float32
BF16 = jnp.bfloat16
LANES = 128
VMEM_LIMIT = 24 * 1024 * 1024


def dot_nn(a, b):
    return lax.dot_general(a, b, (((1,), (0,)), ((), ())), preferred_element_type=F32)


def dot_nt(a, b):
    return lax.dot_general(a, b, (((1,), (1,)), ((), ())), preferred_element_type=F32)


def half_sigmoid(x):
    return 0.5 * jnp.tanh(x) + 0.5


def norm_lanes(x, gain):
    cen = x - jnp.mean(x, axis=1, keepdims=True)
    var = jnp.mean(cen * cen, axis=1, keepdims=True)
    return (cen * lax.rsqrt(var + epsilon) * gain).astype(BF16)


def norm_wide(x, gain_ref):
    cen = x - jnp.mean(x, axis=0, keepdims=True)
    var = jnp.mean(cen * cen, axis=0, keepdims=True)
    unit = cen * lax.rsqrt(var + epsilon)
    return jnp.concatenate(
        [
            (unit[:, c : c + LANES] * gain_ref[...]).astype(BF16)
            for c in range(0, x.shape[1], LANES)
        ],
        axis=1,
    )


def store_operands(pt, index, left_s, right_s):
    ch = pt.shape[0] // 4
    chunks = pt.shape[1] // LANES
    left = half_sigmoid(pt[ch : 2 * ch]) * pt[:ch]
    right = half_sigmoid(pt[3 * ch :]) * pt[2 * ch : 3 * ch]
    for c in range(chunks):
        sl = pl.ds(index * chunks + c, ch, stride=16)
        left_s[sl, :] = left[:, c * LANES : (c + 1) * LANES]
        right_s[sl, :] = right[:, c * LANES : (c + 1) * LANES]


def round_out(parts, out_ref):
    for part, ref in enumerate(parts):
        block = ref[...].reshape(out_ref.shape[0], 16, LANES)
        out_ref[:, 16 * part : 16 * (part + 1), :] = block.astype(BF16)


def send_out(parts, out_s, out_hbm, out_sem):
    pieces = out_sem.shape[0]
    size = out_s.shape[0] // pieces
    copies = []
    for p in range(pieces):
        peers = slice(p * size, (p + 1) * size)
        for part, ref in enumerate(parts):
            block = ref[p * size * 16 : (p + 1) * size * 16, :]
            out_s[peers, 16 * part : 16 * (part + 1), :] = block.reshape(size, 16, LANES).astype(BF16)
        copies.append(pltpu.make_async_copy(out_s.at[peers], out_hbm.at[peers], out_sem.at[p]))
        copies[-1].start()
    for copy in copies:
        copy.wait()


def flip(block, factor=1.0):
    return (block.astype(F32).T * factor).astype(BF16)


def flip_projections(w_ref, update, wt_ref):
    ch = w_ref.shape[2] // 4
    for part in range(4):
        block = w_ref[update, :, part * ch : (part + 1) * ch]
        wt_ref[part * ch : (part + 1) * ch, :] = flip(block, 0.5 if part % 2 else 1.0)


def widen(gain):
    return jnp.broadcast_to(gain, (LANES, gain.shape[1])).T


def prepare_kernel(
    x_hbm, w_hbm, gain_hbm, out_ref, x_ref, w_ref, gain_ref, wt_s, left_s, right_s, state_s, x_s, x_sem, w_sem, gain_sem
):
    rows, tokens, _ = x_ref.shape
    peers = out_ref.shape[0]
    cols = tokens // peers
    w_copy = pltpu.make_async_copy(w_hbm.at[0:1], w_ref, w_sem)
    gain_copy = pltpu.make_async_copy(gain_hbm, gain_ref, gain_sem)
    x_copies = [pltpu.make_async_copy(x_hbm.at[i], x_ref.at[i], x_sem.at[i]) for i in range(rows)]
    w_copy.start()
    gain_copy.start()
    for copy in x_copies:
        copy.start()
    w_copy.wait()
    flip_projections(w_ref, 0, wt_s)
    gain_copy.wait()
    for i in range(rows):
        x_copies[i].wait()
        x = x_ref[i].astype(F32)
        x_s[...] = x
        store_operands(dot_nt(wt_s[...], norm_lanes(x, gain_ref[0:1, :])), i, left_s, right_s)
        for j in range(cols):
            state_s[pl.ds(i * cols + j, peers, stride=16), :] = x_s[pl.ds(j, peers, stride=cols), :]
    round_out((left_s, right_s, state_s), out_ref)


def mix_first_kernel(in_ref, out_hbm, state_ref, *scratch):
    state_ref[...] = in_ref[:, 32:48, :]
    mix_kernel(in_ref, out_hbm, *scratch)


def mix_kernel(in_ref, out_hbm, left_s, right_s, left_b, right_b, out_s, out_sem):
    peers = in_ref.shape[0]
    tokens = left_b.shape[0]
    chunks = tokens // LANES
    for part, (wide, whole) in enumerate(((left_s, left_b), (right_s, right_b))):
        wide[...] = in_ref[:, 16 * part : 16 * (part + 1), :].astype(F32).reshape(peers * 16, LANES)
        for c in range(chunks):
            whole[:, c * LANES : (c + 1) * LANES] = wide[pl.ds(c, tokens, stride=chunks), :].astype(BF16)
    mixed = dot_nt(right_b[...], left_b[...])
    for c in range(chunks):
        left_s[pl.ds(c, tokens, stride=chunks), :] = mixed[:, c * LANES : (c + 1) * LANES]
    send_out((left_s,), out_s, out_hbm, out_sem)


def gate_first_kernel(
    in_ref, w_ref, g_ref, o_ref, igain_ref, hgain_ref, state_ref, gate_ref, wt_ref, gt_ref, ot_ref, iwide_ref, hwide_ref, wide
):
    peers = in_ref.shape[0]
    cols, _, tokens = state_ref.shape
    wide[...] = in_ref[...].astype(F32).reshape(peers * 16, LANES)
    first = flip(g_ref[0], 0.5)
    for j in range(cols):
        x = wide[pl.ds(j, tokens, stride=cols), :]
        normed = norm_lanes(x, igain_ref[0:1, :])
        gate_ref[j] = half_sigmoid(dot_nt(first, normed))
        state_ref[j] = x.T.astype(BF16)
    flip_projections(w_ref, 1, wt_ref)
    gt_ref[...] = flip(g_ref[1], 0.5)
    iwide_ref[...] = widen(igain_ref[1:2, :])
    for update in range(2):
        ot_ref[update] = flip(o_ref[update])
        hwide_ref[update] = widen(hgain_ref[update : update + 1, :])


def gate_second_kernel(state_ref, gt_ref, igain_ref, gate_ref):
    for j in range(state_ref.shape[0]):
        normed = norm_wide(state_ref[j].astype(F32), igain_ref)
        gate_ref[j] = half_sigmoid(dot_nn(gt_ref[...], normed))


def normalize_mixed(mixed_ref, wide):
    y = mixed_ref[...].astype(F32)
    cen = y - jnp.mean(y, axis=0, keepdims=True)
    var = jnp.mean(cen * cen, axis=0, keepdims=True)
    wide[...] = (cen * lax.rsqrt(var + epsilon)).reshape(wide.shape)


def hidden_of(wide, update, j, chunks, gain_ref):
    channels = gain_ref.shape[1]
    return jnp.concatenate(
        [
            (wide[pl.ds(j * chunks + c, channels, stride=16), :] * gain_ref[update]).astype(BF16)
            for c in range(chunks)
        ],
        axis=1,
    )


def middle_kernel(
    mixed_ref, state_ref, gate_ref, hgain_ref, ot_ref, igain_ref, wt_ref, out_ref, next_ref, wide, left_s, right_s
):
    cols, _, tokens = state_ref.shape
    chunks = tokens // LANES
    normalize_mixed(mixed_ref, wide)
    for j in range(cols):
        update = dot_nn(ot_ref[0], hidden_of(wide, 0, j, chunks, hgain_ref))
        state = (state_ref[j].astype(F32) + gate_ref[j] * update).astype(BF16)
        next_ref[j] = state
        normed = norm_wide(state.astype(F32), igain_ref)
        store_operands(dot_nn(wt_ref[...], normed), j, left_s, right_s)
    round_out((left_s, right_s), out_ref)


def last_kernel(mixed_ref, state_ref, gate_ref, hgain_ref, ot_ref, out_ref, wide, out_s):
    cols, _, tokens = state_ref.shape
    chunks = tokens // LANES
    normalize_mixed(mixed_ref, wide)
    for j in range(cols):
        update = dot_nn(ot_ref[1], hidden_of(wide, 1, j, chunks, hgain_ref))
        state = (state_ref[j].astype(F32) + gate_ref[j] * update).astype(BF16)
        out_s[pl.ds(j, tokens, stride=cols), :] = state.T.astype(F32)
    out_ref[...] = out_s[...].astype(BF16)


def call(kernel, out_shape, scratch, flops, moved, args, limit=VMEM_LIMIT, **options):
    return pl.pallas_call(
        kernel,
        out_shape=out_shape,
        scratch_shapes=[pltpu.VMEM(*spec) if isinstance(spec, tuple) else spec for spec in scratch],
        compiler_params=pltpu.CompilerParams(vmem_limit_bytes=limit),
        cost_estimate=pl.CostEstimate(flops=flops, bytes_accessed=moved, transcendentals=0),
        name=kernel.__name__,
        **options,
    )(*args)


def exchange(buffer):
    return lax.all_to_all(buffer, AXES, split_axis=0, concat_axis=0, tiled=True)


def on_device(pair_state, input_weights, gate_weights, output_weights, input_gains, hidden_gains):
    rows, tokens, cp = pair_state.shape
    ch = output_weights.shape[1]
    peers = tokens // rows
    shape = jax.ShapeDtypeStruct
    positions = rows * tokens
    wide = ((positions, LANES), F32)
    whole = ((tokens, tokens), BF16)
    size = positions * ch * 2
    project = 2 * positions * cp * 4 * ch
    small = 2 * positions * cp * ch
    packed = shape((peers, 16, LANES), BF16)
    mix = functools.partial(
        call,
        scratch=[wide, wide, whole, whole, ((peers, 16, LANES), BF16), pltpu.SemaphoreType.DMA((4,))],
        flops=2 * tokens**3,
        moved=3 * size,
    )
    transposed = shape((rows, cp, tokens), BF16)
    gating = shape((rows, cp, tokens), F32)

    in_hbm, in_vmem = (pl.BlockSpec(memory_space=m) for m in (pltpu.HBM, pltpu.VMEM))
    sent = call(
        prepare_kernel,
        shape((peers, 48, LANES), BF16),
        [
            ((rows, tokens, cp), BF16),
            ((1, cp, 4 * ch), BF16),
            ((2, cp), F32),
            ((4 * ch, cp), BF16),
            wide,
            wide,
            wide,
            ((tokens, cp), F32),
            pltpu.SemaphoreType.DMA((rows,)),
            pltpu.SemaphoreType.DMA,
            pltpu.SemaphoreType.DMA,
        ],
        project,
        4 * size,
        args=[
            pltpu.with_memory_space_constraint(a, pltpu.HBM)
            for a in (pair_state, input_weights, input_gains)
        ],
        in_specs=[in_hbm] * 3,
    )
    mixed, state = mix(
        mix_first_kernel, (packed, packed), args=(exchange(sent),), out_specs=(in_hbm, in_vmem)
    )
    mixed = exchange(mixed)
    state, gate, wt, gt, ot, iwide, hwide = call(
        gate_first_kernel,
        (
            transposed,
            gating,
            shape((4 * ch, cp), BF16),
            shape((cp, cp), BF16),
            shape((2, cp, ch), BF16),
            shape((cp, LANES), F32),
            shape((2, ch, LANES), F32),
        ),
        [wide],
        2 * small,
        5 * size,
        args=(state, input_weights, gate_weights, output_weights, input_gains, hidden_gains),
    )
    sent, state = call(
        middle_kernel,
        (shape((peers, 32, LANES), BF16), transposed),
        [wide, wide, wide],
        project + small,
        6 * size,
        args=(mixed, state, gate, hwide, ot, iwide, wt),
    )
    mixed = exchange(mix(mix_kernel, packed, args=(exchange(sent),), out_specs=in_hbm))
    gate = call(gate_second_kernel, gating, [], small, 3 * size, (state, gt, iwide))
    out = call(
        last_kernel,
        shape((positions, cp), BF16),
        [wide, wide],
        small,
        5 * size,
        args=(mixed, state, gate, hwide, ot),
    )
    return out.reshape(tokens, rows, cp)


def solution(mesh):
    return jax.shard_map(
        on_device,
        mesh=mesh,
        in_specs=(P(AXES, None, None), P(), P(), P(), P(), P()),
        out_specs=P(None, AXES, None),
        check_vma=False,
    )
```

```python
import jax
import jax.numpy as jnp
from jax import lax
from jax.experimental import pallas as pl
from jax.experimental.pallas import tpu as pltpu
from jax.sharding import PartitionSpec as P

epsilon = 1e-05
AXES = ("dap", "rep")
F32 = jnp.float32
BF16 = jnp.bfloat16
LANES = 128
ROWS = 4
VMEM_LIMIT = 24 * 1024 * 1024


def dot_nn(a, b):
    return lax.dot_general(a, b, (((1,), (0,)), ((), ())), preferred_element_type=F32)


def dot_nt(a, b):
    return lax.dot_general(a, b, (((1,), (1,)), ((), ())), preferred_element_type=F32)


def half_sigmoid(x):
    return 0.5 * jnp.tanh(x) + 0.5


def norm_lanes(x, gain):
    cen = x - jnp.mean(x, axis=1, keepdims=True)
    var = jnp.mean(cen * cen, axis=1, keepdims=True)
    return (cen * lax.rsqrt(var + epsilon) * gain).astype(BF16)


def norm_wide(x, gain_ref):
    cen = x - jnp.mean(x, axis=0, keepdims=True)
    var = jnp.mean(cen * cen, axis=0, keepdims=True)
    unit = cen * lax.rsqrt(var + epsilon)
    return jnp.concatenate(
        [
            (unit[:, c : c + LANES] * gain_ref[...]).astype(BF16)
            for c in range(0, x.shape[1], LANES)
        ],
        axis=1,
    )


def store_operands(pt, index, rows, left_s, right_s):
    ch = pt.shape[0] // 4
    chunks = pt.shape[1] // LANES
    left = half_sigmoid(pt[ch : 2 * ch]) * pt[:ch]
    right = half_sigmoid(pt[3 * ch :]) * pt[2 * ch : 3 * ch]
    for c in range(chunks):
        sl = pl.ds(c * rows + index, ch, stride=16)
        left_s[sl, :] = left[:, c * LANES : (c + 1) * LANES]
        right_s[sl, :] = right[:, c * LANES : (c + 1) * LANES]


def round_out(parts, out_ref):
    for part, ref in enumerate(parts):
        block = ref[...].reshape(out_ref.shape[0], 16, LANES)
        out_ref[:, 16 * part : 16 * (part + 1), :] = block.astype(BF16)


def flip(block, factor=1.0):
    return (block.astype(F32).T * factor).astype(BF16)


def flip_projections(w_ref, update, wt_ref):
    ch = w_ref.shape[2] // 4
    for part in range(4):
        block = w_ref[update, :, part * ch : (part + 1) * ch]
        wt_ref[part * ch : (part + 1) * ch, :] = flip(block, 0.5 if part % 2 else 1.0)


def widen(gain):
    return jnp.broadcast_to(gain, (LANES, gain.shape[1])).T


def prepare_kernel(x_hbm, w_hbm, gain_hbm, out_ref, x_ref, w_ref, gain_ref, wt_s, left_s, right_s, sem):
    rows, tokens, _ = x_ref.shape
    peers = out_ref.shape[0]
    cols = tokens // peers
    copies = [
        pltpu.make_async_copy(w_hbm.at[0:1], w_ref, sem.at[0]),
        pltpu.make_async_copy(x_hbm, x_ref, sem.at[1]),
        pltpu.make_async_copy(gain_hbm, gain_ref, sem.at[2]),
    ]
    for copy in copies:
        copy.start()
    for copy in copies:
        copy.wait()
    flip_projections(w_ref, 0, wt_s)
    for i in range(rows):
        x = x_ref[i].astype(F32)
        normed = norm_lanes(x, gain_ref[0:1, :])
        store_operands(dot_nt(wt_s[...], normed), i, rows, left_s, right_s)
    round_out((left_s, right_s), out_ref)
    state = [x_ref[i].astype(F32).reshape(peers, cols, LANES) for i in range(rows)]
    out_ref[:, 32:48, :] = jnp.concatenate(state, axis=1).astype(BF16)


def gathered(in_ref, part, rows):
    peers = in_ref.shape[0]
    block = in_ref[:, 16 * part : 16 * (part + 1), :].astype(F32)
    return jnp.concatenate(
        [
            block[:, r : r + rows, :].reshape(peers * rows, LANES).astype(BF16)
            for r in range(0, 16, rows)
        ],
        axis=1,
    )


def mix_kernel(in_ref, out_ref):
    peers = in_ref.shape[0]
    rows = ROWS
    mixed = dot_nt(gathered(in_ref, 1, rows), gathered(in_ref, 0, rows))
    blocks = [
        mixed[:, c * LANES : (c + 1) * LANES].reshape(peers, rows, LANES) for c in range(16 // rows)
    ]
    out_ref[...] = jnp.concatenate(blocks, axis=1).astype(BF16)


def mix_first_kernel(
    in_ref,
    w_ref,
    g_ref,
    o_ref,
    igain_ref,
    hgain_ref,
    out_ref,
    state_ref,
    gate_ref,
    wt_ref,
    gt_ref,
    ot_ref,
    iwide_ref,
    hwide_ref,
    wide,
):
    peers = in_ref.shape[0]
    cols, _, tokens = state_ref.shape
    wide[...] = in_ref[:, 32:48, :].astype(F32).reshape(peers * 16, LANES)
    mix_kernel(in_ref, out_ref)
    first = flip(g_ref[0], 0.5)
    for j in range(cols):
        x = wide[pl.ds(j, tokens, stride=cols), :]
        normed = norm_lanes(x, igain_ref[0:1, :])
        gate_ref[j] = half_sigmoid(dot_nt(first, normed))
        state_ref[j] = x.T.astype(BF16)
    flip_projections(w_ref, 1, wt_ref)
    gt_ref[...] = flip(g_ref[1], 0.5)
    iwide_ref[...] = widen(igain_ref[1:2, :])
    for update in range(2):
        ot_ref[update] = flip(o_ref[update])
        hwide_ref[update] = widen(hgain_ref[update : update + 1, :])


def normalize_mixed(mixed_ref, wide):
    y = mixed_ref[...].astype(F32)
    cen = y - jnp.mean(y, axis=0, keepdims=True)
    var = jnp.mean(cen * cen, axis=0, keepdims=True)
    wide[...] = (cen * lax.rsqrt(var + epsilon)).reshape(wide.shape)


def hidden_of(wide, update, j, cols, chunks, gain_ref):
    channels = gain_ref.shape[1]
    return jnp.concatenate(
        [
            (wide[pl.ds(c * cols + j, channels, stride=16), :] * gain_ref[update]).astype(BF16)
            for c in range(chunks)
        ],
        axis=1,
    )


def middle_kernel(
    mixed_ref, state_ref, gate_ref, hgain_ref, ot_ref, igain_ref, wt_ref, out_ref, next_ref, wide, left_s, right_s
):
    cols, _, tokens = state_ref.shape
    chunks = tokens // LANES
    normalize_mixed(mixed_ref, wide)
    for j in range(cols):
        update = dot_nn(ot_ref[0], hidden_of(wide, 0, j, cols, chunks, hgain_ref))
        state = (state_ref[j].astype(F32) + gate_ref[j] * update).astype(BF16)
        next_ref[j] = state
        normed = norm_wide(state.astype(F32), igain_ref)
        store_operands(dot_nn(wt_ref[...], normed), j, cols, left_s, right_s)
    round_out((left_s, right_s), out_ref)


def last_kernel(mixed_ref, state_ref, gt_ref, igain_ref, hgain_ref, ot_ref, out_ref, wide, out_s):
    cols, _, tokens = state_ref.shape
    chunks = tokens // LANES
    normalize_mixed(mixed_ref, wide)
    for j in range(cols):
        update = dot_nn(ot_ref[1], hidden_of(wide, 1, j, cols, chunks, hgain_ref))
        old = state_ref[j].astype(F32)
        gate = half_sigmoid(dot_nn(gt_ref[...], norm_wide(old, igain_ref)))
        state = (old + gate * update).astype(BF16)
        out_s[pl.ds(j, tokens, stride=cols), :] = state.T.astype(F32)
    out_ref[...] = out_s[...].astype(BF16)


def call(kernel, out_shape, scratch, flops, moved, args, limit=VMEM_LIMIT, **options):
    return pl.pallas_call(
        kernel,
        out_shape=out_shape,
        scratch_shapes=[pltpu.VMEM(*spec) if isinstance(spec, tuple) else spec for spec in scratch],
        compiler_params=pltpu.CompilerParams(vmem_limit_bytes=limit),
        cost_estimate=pl.CostEstimate(flops=flops, bytes_accessed=moved, transcendentals=0),
        name=kernel.__name__,
        **options,
    )(*args)


def exchange(buffer):
    return lax.all_to_all(buffer, AXES, split_axis=0, concat_axis=0, tiled=True)


def on_device(pair_state, input_weights, gate_weights, output_weights, input_gains, hidden_gains):
    rows, tokens, cp = pair_state.shape
    ch = output_weights.shape[1]
    peers = tokens // rows
    shape = jax.ShapeDtypeStruct
    positions = rows * tokens
    wide = ((positions, LANES), F32)
    size = positions * ch * 2
    project = 2 * positions * cp * 4 * ch
    small = 2 * positions * cp * ch
    mixing = 2 * tokens**3
    packed = shape((peers, 16, LANES), BF16)
    transposed = shape((rows, cp, tokens), BF16)

    sent = call(
        prepare_kernel,
        shape((peers, 48, LANES), BF16),
        [
            ((rows, tokens, cp), BF16),
            ((1, cp, 4 * ch), BF16),
            ((2, cp), F32),
            ((4 * ch, cp), BF16),
            wide,
            wide,
            pltpu.SemaphoreType.DMA((3,)),
        ],
        project,
        4 * size,
        args=[
            pltpu.with_memory_space_constraint(a, pltpu.HBM)
            for a in (pair_state, input_weights, input_gains)
        ],
        in_specs=[pl.BlockSpec(memory_space=pltpu.HBM)] * 3,
    )
    mixed, state, gate, wt, gt, ot, iwide, hwide = call(
        mix_first_kernel,
        (
            packed,
            transposed,
            shape((rows, cp, tokens), F32),
            shape((4 * ch, cp), BF16),
            shape((cp, cp), BF16),
            shape((2, cp, ch), BF16),
            shape((cp, LANES), F32),
            shape((2, ch, LANES), F32),
        ),
        [wide],
        mixing + 2 * small,
        7 * size,
        args=(
            exchange(sent),
            input_weights,
            gate_weights,
            output_weights,
            input_gains,
            hidden_gains,
        ),
    )
    sent, state = call(
        middle_kernel,
        (shape((peers, 32, LANES), BF16), transposed),
        [wide, wide, wide],
        project + small,
        6 * size,
        args=(exchange(mixed), state, gate, hwide, ot, iwide, wt),
    )
    mixed = call(mix_kernel, packed, [], mixing, 3 * size, args=(exchange(sent),))
    out = call(
        last_kernel,
        shape((positions, cp), BF16),
        [wide, wide],
        2 * small,
        3 * size,
        args=(exchange(mixed), state, gt, iwide, hwide, ot),
    )
    return out.reshape(tokens, rows, cp)


def solution(mesh):
    return jax.shard_map(
        on_device,
        mesh=mesh,
        in_specs=(P(AXES, None, None), P(), P(), P(), P(), P()),
        out_specs=P(None, AXES, None),
        check_vma=False,
    )
```

```python
import jax
import jax.numpy as jnp
from jax import lax
from jax.experimental import pallas as pl
from jax.experimental.pallas import tpu as pltpu
from jax.sharding import PartitionSpec as P

epsilon = 1e-05
AXES = ("dap", "rep")
F32 = jnp.float32
BF16 = jnp.bfloat16
LANES = 128
ROWS = 4
PITCH = 24
VMEM_LIMIT = 24 * 1024 * 1024


def dot_nn(a, b):
    return lax.dot_general(a, b, (((1,), (0,)), ((), ())), preferred_element_type=F32)


def dot_nt(a, b):
    return lax.dot_general(a, b, (((1,), (1,)), ((), ())), preferred_element_type=F32)


def half_sigmoid(x):
    return 0.5 * jnp.tanh(x) + 0.5


def norm_lanes(x, gain):
    cen = x - jnp.mean(x, axis=1, keepdims=True)
    var = jnp.mean(cen * cen, axis=1, keepdims=True)
    return (cen * lax.rsqrt(var + epsilon) * gain).astype(BF16)


def norm_wide(x, gain_ref):
    cen = x - jnp.mean(x, axis=0, keepdims=True)
    var = jnp.mean(cen * cen, axis=0, keepdims=True)
    unit = cen * lax.rsqrt(var + epsilon)
    return jnp.concatenate(
        [
            (unit[:, c : c + LANES] * gain_ref[...]).astype(BF16)
            for c in range(0, x.shape[1], LANES)
        ],
        axis=1,
    )


def store_operands(pt, index, rows, left_s, right_s):
    ch = pt.shape[0] // 4
    chunks = pt.shape[1] // LANES
    left = half_sigmoid(pt[ch : 2 * ch]) * pt[:ch]
    right = half_sigmoid(pt[3 * ch :]) * pt[2 * ch : 3 * ch]
    for c in range(chunks):
        sl = pl.ds(c * rows + index, ch, stride=PITCH)
        left_s[sl, :] = left[:, c * LANES : (c + 1) * LANES]
        right_s[sl, :] = right[:, c * LANES : (c + 1) * LANES]


def round_out(parts, out_ref):
    for part, ref in enumerate(parts):
        block = ref[...].reshape(out_ref.shape[0], PITCH, LANES)[:, :16, :]
        out_ref[:, 16 * part : 16 * (part + 1), :] = block.astype(BF16)


def flip(block, factor=1.0):
    return (block.astype(F32).T * factor).astype(BF16)


def flip_projections(w_ref, update, wt_ref):
    ch = w_ref.shape[2] // 4
    for part in range(4):
        block = w_ref[update, :, part * ch : (part + 1) * ch]
        wt_ref[part * ch : (part + 1) * ch, :] = flip(block, 0.5 if part % 2 else 1.0)


def widen(gain):
    return jnp.broadcast_to(gain, (LANES, gain.shape[1])).T


def prepare_kernel(x_hbm, w_hbm, gain_hbm, out_ref, x_ref, w_ref, gain_ref, wt_s, left_s, right_s, sem):
    rows, tokens, _ = x_ref.shape
    peers = out_ref.shape[0]
    cols = tokens // peers
    copies = [
        pltpu.make_async_copy(w_hbm.at[0:1], w_ref, sem.at[0]),
        pltpu.make_async_copy(x_hbm, x_ref, sem.at[1]),
        pltpu.make_async_copy(gain_hbm, gain_ref, sem.at[2]),
    ]
    for copy in copies:
        copy.start()
    for copy in copies:
        copy.wait()
    flip_projections(w_ref, 0, wt_s)
    normed = [norm_lanes(x_ref[i].astype(F32), gain_ref[0:1, :]) for i in range(rows)]
    state = [x_ref[i].astype(F32).reshape(peers, cols, LANES) for i in range(rows)]
    out_ref[:, 32:48, :] = jnp.concatenate(state, axis=1).astype(BF16)
    for i in range(rows):
        store_operands(dot_nt(wt_s[...], normed[i]), i, rows, left_s, right_s)
    round_out((left_s, right_s), out_ref)


def gathered(in_ref, part, rows):
    peers = in_ref.shape[0]
    block = in_ref[:, 16 * part : 16 * (part + 1), :].astype(F32)
    return jnp.concatenate(
        [
            block[:, r : r + rows, :].reshape(peers * rows, LANES).astype(BF16)
            for r in range(0, 16, rows)
        ],
        axis=1,
    )


def mix_kernel(in_ref, out_ref):
    peers = in_ref.shape[0]
    rows = ROWS
    mixed = dot_nt(gathered(in_ref, 1, rows), gathered(in_ref, 0, rows))
    blocks = [
        mixed[:, c * LANES : (c + 1) * LANES].reshape(peers, rows, LANES) for c in range(16 // rows)
    ]
    out_ref[...] = jnp.concatenate(blocks, axis=1).astype(BF16)


def mix_first_kernel(
    in_ref,
    w_ref,
    g_ref,
    o_ref,
    igain_ref,
    hgain_ref,
    out_ref,
    state_ref,
    gate_ref,
    wt_ref,
    gt_ref,
    ot_ref,
    iwide_ref,
    hwide_ref,
    wide,
):
    peers = in_ref.shape[0]
    cols, _, tokens = state_ref.shape
    wide[...] = in_ref[:, 32:48, :].astype(F32).reshape(peers * 16, LANES)
    mix_kernel(in_ref, out_ref)
    first = flip(g_ref[0], 0.5)
    for j in range(cols):
        x = wide[pl.ds(j, tokens, stride=cols), :]
        normed = norm_lanes(x, igain_ref[0:1, :])
        gate_ref[j] = half_sigmoid(dot_nt(first, normed))
        state_ref[j] = x.T.astype(BF16)
    flip_projections(w_ref, 1, wt_ref)
    gt_ref[...] = flip(g_ref[1], 0.5)
    iwide_ref[...] = widen(igain_ref[1:2, :])
    for update in range(2):
        ot_ref[update] = flip(o_ref[update])
        hwide_ref[update] = widen(hgain_ref[update : update + 1, :])


def normalize_mixed(mixed_ref, wide):
    y = mixed_ref[...].astype(F32)
    cen = y - jnp.mean(y, axis=0, keepdims=True)
    var = jnp.mean(cen * cen, axis=0, keepdims=True)
    unit = cen * lax.rsqrt(var + epsilon)
    for h in range(unit.shape[0]):
        wide[PITCH * h : PITCH * h + 16, :] = unit[h]


def hidden_of(wide, j, cols, chunks, gain):
    return jnp.concatenate(
        [
            (wide[pl.ds(c * cols + j, gain.shape[0], stride=PITCH), :] * gain).astype(BF16)
            for c in chunks
        ],
        axis=1,
    )


def middle_kernel(
    mixed_ref, state_ref, gate_ref, hgain_ref, ot_ref, igain_ref, wt_ref, out_ref, next_ref, wide, left_s, right_s
):
    cols, _, tokens = state_ref.shape
    chunks = range(tokens // LANES)
    normalize_mixed(mixed_ref, wide)
    normed = []
    for j in range(cols):
        update = dot_nn(ot_ref[0], hidden_of(wide, j, cols, chunks, hgain_ref[0]))
        state = (state_ref[j].astype(F32) + gate_ref[j] * update).astype(BF16)
        next_ref[j] = state
        normed.append(norm_wide(state.astype(F32), igain_ref))
    for j in range(cols):
        store_operands(dot_nn(wt_ref[...], normed[j]), j, cols, left_s, right_s)
    round_out((left_s, right_s), out_ref)


def last_kernel(mixed_ref, state_ref, gt_ref, igain_ref, hgain_ref, ot_ref, out_hbm, wide, out_s, out_b, sem):
    cols, _, tokens = state_ref.shape
    parts = sem.shape[0]
    size = tokens // parts
    chunks = size // LANES
    normalize_mixed(mixed_ref, wide)
    copies = []
    for p in range(parts):
        for j in range(cols):
            old = state_ref[j, :, p * size : (p + 1) * size].astype(F32)
            hidden = hidden_of(wide, j, cols, range(p * chunks, (p + 1) * chunks), hgain_ref[1])
            gate = half_sigmoid(dot_nn(gt_ref[...], norm_wide(old, igain_ref)))
            state = (old + gate * dot_nn(ot_ref[1], hidden)).astype(BF16)
            out_s[pl.ds(p * size * cols + j, size, stride=cols), :] = state.T.astype(F32)
        block = slice(p * size * cols, (p + 1) * size * cols)
        out_b[block, :] = out_s[block, :].astype(BF16)
        copies.append(pltpu.make_async_copy(out_b.at[block], out_hbm.at[block], sem.at[p]))
        copies[-1].start()
    for copy in copies:
        copy.wait()


def call(kernel, out_shape, scratch, flops, moved, args, limit=VMEM_LIMIT, **options):
    return pl.pallas_call(
        kernel,
        out_shape=out_shape,
        scratch_shapes=[pltpu.VMEM(*spec) if isinstance(spec, tuple) else spec for spec in scratch],
        compiler_params=pltpu.CompilerParams(vmem_limit_bytes=limit),
        cost_estimate=pl.CostEstimate(flops=flops, bytes_accessed=moved, transcendentals=0),
        name=kernel.__name__,
        **options,
    )(*args)


def exchange(buffer):
    return lax.all_to_all(buffer, AXES, split_axis=0, concat_axis=0, tiled=True)


def on_device(pair_state, input_weights, gate_weights, output_weights, input_gains, hidden_gains):
    rows, tokens, cp = pair_state.shape
    ch = output_weights.shape[1]
    peers = tokens // rows
    shape = jax.ShapeDtypeStruct
    positions = rows * tokens
    wide = ((positions, LANES), F32)
    pitched = ((peers * PITCH, LANES), F32)
    size = positions * ch * 2
    project = 2 * positions * cp * 4 * ch
    small = 2 * positions * cp * ch
    mixing = 2 * tokens**3
    packed = shape((peers, 16, LANES), BF16)
    transposed = shape((rows, cp, tokens), BF16)

    sent = call(
        prepare_kernel,
        shape((peers, 48, LANES), BF16),
        [
            ((rows, tokens, cp), BF16),
            ((1, cp, 4 * ch), BF16),
            ((2, cp), F32),
            ((4 * ch, cp), BF16),
            pitched,
            pitched,
            pltpu.SemaphoreType.DMA((3,)),
        ],
        project,
        4 * size,
        args=[
            pltpu.with_memory_space_constraint(a, pltpu.HBM)
            for a in (pair_state, input_weights, input_gains)
        ],
        in_specs=[pl.BlockSpec(memory_space=pltpu.HBM)] * 3,
    )
    mixed, state, gate, wt, gt, ot, iwide, hwide = call(
        mix_first_kernel,
        (
            packed,
            transposed,
            shape((rows, cp, tokens), F32),
            shape((4 * ch, cp), BF16),
            shape((cp, cp), BF16),
            shape((2, cp, ch), BF16),
            shape((cp, LANES), F32),
            shape((2, ch, LANES), F32),
        ),
        [wide],
        mixing + 2 * small,
        7 * size,
        args=(
            exchange(sent),
            input_weights,
            gate_weights,
            output_weights,
            input_gains,
            hidden_gains,
        ),
    )
    sent, state = call(
        middle_kernel,
        (shape((peers, 32, LANES), BF16), transposed),
        [pitched, pitched, pitched],
        project + small,
        6 * size,
        args=(exchange(mixed), state, gate, hwide, ot, iwide, wt),
    )
    mixed = call(mix_kernel, packed, [], mixing, 3 * size, args=(exchange(sent),))
    out = call(
        last_kernel,
        shape((positions, cp), BF16),
        [pitched, wide, ((positions, LANES), BF16), pltpu.SemaphoreType.DMA((2,))],
        2 * small,
        3 * size,
        args=(exchange(mixed), state, gt, iwide, hwide, ot),
        out_specs=pl.BlockSpec(memory_space=pltpu.HBM),
    )
    return out.reshape(tokens, rows, cp)


def solution(mesh):
    return jax.shard_map(
        on_device,
        mesh=mesh,
        in_specs=(P(AXES, None, None), P(), P(), P(), P(), P()),
        out_specs=P(None, AXES, None),
        check_vma=False,
    )
```

```python
import jax
import jax.numpy as jnp
from jax import lax
from jax.experimental import pallas as pl
from jax.experimental.pallas import tpu as pltpu
from jax.sharding import PartitionSpec as P

epsilon = 1e-05
AXES = ("dap", "rep")
F32 = jnp.float32
BF16 = jnp.bfloat16
LANES = 128
ROWS = 4
PITCH = 24
VMEM_LIMIT = 24 * 1024 * 1024


def dot_nn(a, b):
    return lax.dot_general(a, b, (((1,), (0,)), ((), ())), preferred_element_type=F32)


def dot_nt(a, b):
    return lax.dot_general(a, b, (((1,), (1,)), ((), ())), preferred_element_type=F32)


def half_sigmoid(x):
    return 0.5 * jnp.tanh(x) + 0.5


def norm_wide(x, gain_ref):
    cen = x - jnp.mean(x, axis=0, keepdims=True)
    var = jnp.mean(cen * cen, axis=0, keepdims=True)
    unit = cen * lax.rsqrt(var + epsilon)
    return jnp.concatenate(
        [
            (unit[:, c : c + LANES] * gain_ref[...]).astype(BF16)
            for c in range(0, x.shape[1], LANES)
        ],
        axis=1,
    )


def store_operands(pt, index, rows, left_s, right_s):
    ch = pt.shape[0] // 4
    chunks = pt.shape[1] // LANES
    left = half_sigmoid(pt[ch : 2 * ch]) * pt[:ch]
    right = half_sigmoid(pt[3 * ch :]) * pt[2 * ch : 3 * ch]
    for c in range(chunks):
        sl = pl.ds(c * rows + index, ch, stride=PITCH)
        left_s[sl, :] = left[:, c * LANES : (c + 1) * LANES]
        right_s[sl, :] = right[:, c * LANES : (c + 1) * LANES]


def round_out(parts, out_ref):
    for part, ref in enumerate(parts):
        block = ref[...].reshape(out_ref.shape[0], PITCH, LANES)[:, :16, :]
        out_ref[:, 16 * part : 16 * (part + 1), :] = block.astype(BF16)


def flip(block, factor=1.0):
    return (block.astype(F32).T * factor).astype(BF16)


def flip_projections(w_ref, update, wt_ref):
    ch = w_ref.shape[2] // 4
    for part in range(4):
        block = w_ref[update, :, part * ch : (part + 1) * ch]
        wt_ref[part * ch : (part + 1) * ch, :] = flip(block, 0.5 if part % 2 else 1.0)


def widen(gain):
    return jnp.broadcast_to(gain, (LANES, gain.shape[1])).T


def prepare_kernel(x_hbm, w_hbm, gain_hbm, out_ref, x_ref, w_ref, gain_ref, wt_s, wide_s, left_s, right_s, sem):
    rows, tokens, _ = x_ref.shape
    peers = out_ref.shape[0]
    cols = tokens // peers
    copies = [
        pltpu.make_async_copy(w_hbm.at[0:1], w_ref, sem.at[0]),
        pltpu.make_async_copy(x_hbm, x_ref, sem.at[1]),
        pltpu.make_async_copy(gain_hbm, gain_ref, sem.at[2]),
    ]
    for copy in copies:
        copy.start()
    for copy in copies:
        copy.wait()
    flip_projections(w_ref, 0, wt_s)
    wide_s[...] = widen(gain_ref[0:1, :])
    normed = [norm_wide(x_ref[i].T.astype(F32), wide_s) for i in range(rows)]
    state = [x_ref[i].astype(F32).reshape(peers, cols, LANES) for i in range(rows)]
    out_ref[:, 32:48, :] = jnp.concatenate(state, axis=1).astype(BF16)
    for i in range(rows):
        store_operands(dot_nn(wt_s[...], normed[i]), i, rows, left_s, right_s)
    round_out((left_s, right_s), out_ref)


def gathered(in_ref, part, rows):
    peers = in_ref.shape[0]
    block = in_ref[:, 16 * part : 16 * (part + 1), :].astype(F32)
    return jnp.concatenate(
        [
            block[:, r : r + rows, :].reshape(peers * rows, LANES).astype(BF16)
            for r in range(0, 16, rows)
        ],
        axis=1,
    )


def mix_kernel(in_ref, out_ref):
    peers = in_ref.shape[0]
    rows = ROWS
    mixed = dot_nt(gathered(in_ref, 1, rows), gathered(in_ref, 0, rows))
    blocks = [
        mixed[:, c * LANES : (c + 1) * LANES].reshape(peers, rows, LANES) for c in range(16 // rows)
    ]
    out_ref[...] = jnp.concatenate(blocks, axis=1).astype(BF16)


def mix_first_kernel(
    in_ref,
    w_ref,
    g_ref,
    o_ref,
    igain_ref,
    hgain_ref,
    out_ref,
    state_ref,
    gate_ref,
    wt_ref,
    gt_ref,
    ot_ref,
    iwide_ref,
    hwide_ref,
    wide,
    first_s,
):
    peers = in_ref.shape[0]
    cols, _, tokens = state_ref.shape
    wide[...] = in_ref[:, 32:48, :].astype(F32).reshape(peers * 16, LANES)
    mix_kernel(in_ref, out_ref)
    first = flip(g_ref[0], 0.5)
    first_s[...] = widen(igain_ref[0:1, :])
    normed = []
    for j in range(cols):
        state = wide[pl.ds(j, tokens, stride=cols), :].astype(BF16).T
        state_ref[j] = state
        normed.append(norm_wide(state.astype(F32), first_s))
    for j in range(cols):
        gate_ref[j] = half_sigmoid(dot_nn(first, normed[j]))
    flip_projections(w_ref, 1, wt_ref)
    gt_ref[...] = flip(g_ref[1], 0.5)
    iwide_ref[...] = widen(igain_ref[1:2, :])
    for update in range(2):
        ot_ref[update] = flip(o_ref[update])
        hwide_ref[update] = widen(hgain_ref[update : update + 1, :])


def normalize_mixed(mixed_ref, wide):
    y = mixed_ref[...].astype(F32)
    cen = y - jnp.mean(y, axis=0, keepdims=True)
    var = jnp.mean(cen * cen, axis=0, keepdims=True)
    unit = cen * lax.rsqrt(var + epsilon)
    for h in range(unit.shape[0]):
        wide[PITCH * h : PITCH * h + 16, :] = unit[h]


def hidden_of(wide, j, cols, chunks, gain):
    return jnp.concatenate(
        [
            (wide[pl.ds(c * cols + j, gain.shape[0], stride=PITCH), :] * gain).astype(BF16)
            for c in chunks
        ],
        axis=1,
    )


def middle_kernel(
    mixed_ref, state_ref, gate_ref, hgain_ref, ot_ref, igain_ref, wt_ref, out_ref, next_ref, wide, left_s, right_s
):
    cols, _, tokens = state_ref.shape
    chunks = range(tokens // LANES)
    normalize_mixed(mixed_ref, wide)
    normed = []
    for j in range(cols):
        update = dot_nn(ot_ref[0], hidden_of(wide, j, cols, chunks, hgain_ref[0]))
        state = (state_ref[j].astype(F32) + gate_ref[j] * update).astype(BF16)
        next_ref[j] = state
        normed.append(norm_wide(state.astype(F32), igain_ref))
    for j in range(cols):
        store_operands(dot_nn(wt_ref[...], normed[j]), j, cols, left_s, right_s)
    round_out((left_s, right_s), out_ref)


def last_kernel(mixed_ref, state_ref, gt_ref, igain_ref, hgain_ref, ot_ref, out_hbm, wide, out_s, out_b, sem):
    cols, _, tokens = state_ref.shape
    parts = sem.shape[0]
    size = tokens // parts
    chunks = size // LANES
    normalize_mixed(mixed_ref, wide)
    copies = []
    for p in range(parts):
        for j in range(cols):
            old = state_ref[j, :, p * size : (p + 1) * size].astype(F32)
            hidden = hidden_of(wide, j, cols, range(p * chunks, (p + 1) * chunks), hgain_ref[1])
            gate = half_sigmoid(dot_nn(gt_ref[...], norm_wide(old, igain_ref)))
            state = (old + gate * dot_nn(ot_ref[1], hidden)).astype(BF16)
            out_s[pl.ds(p * size * cols + j, size, stride=cols), :] = state.T.astype(F32)
        block = slice(p * size * cols, (p + 1) * size * cols)
        out_b[block, :] = out_s[block, :].astype(BF16)
        copies.append(pltpu.make_async_copy(out_b.at[block], out_hbm.at[block], sem.at[p]))
        copies[-1].start()
    for copy in copies:
        copy.wait()


def call(kernel, out_shape, scratch, flops, moved, args, limit=VMEM_LIMIT, **options):
    return pl.pallas_call(
        kernel,
        out_shape=out_shape,
        scratch_shapes=[pltpu.VMEM(*spec) if isinstance(spec, tuple) else spec for spec in scratch],
        compiler_params=pltpu.CompilerParams(vmem_limit_bytes=limit),
        cost_estimate=pl.CostEstimate(flops=flops, bytes_accessed=moved, transcendentals=0),
        name=kernel.__name__,
        **options,
    )(*args)


def exchange(buffer):
    return lax.all_to_all(buffer, AXES, split_axis=0, concat_axis=0, tiled=True)


def on_device(pair_state, input_weights, gate_weights, output_weights, input_gains, hidden_gains):
    rows, tokens, cp = pair_state.shape
    ch = output_weights.shape[1]
    peers = tokens // rows
    shape = jax.ShapeDtypeStruct
    positions = rows * tokens
    wide = ((positions, LANES), F32)
    pitched = ((peers * PITCH, LANES), F32)
    size = positions * ch * 2
    project = 2 * positions * cp * 4 * ch
    small = 2 * positions * cp * ch
    mixing = 2 * tokens**3
    packed = shape((peers, 16, LANES), BF16)
    transposed = shape((rows, cp, tokens), BF16)

    sent = call(
        prepare_kernel,
        shape((peers, 48, LANES), BF16),
        [
            ((rows, tokens, cp), BF16),
            ((1, cp, 4 * ch), BF16),
            ((2, cp), F32),
            ((4 * ch, cp), BF16),
            ((cp, LANES), F32),
            pitched,
            pitched,
            pltpu.SemaphoreType.DMA((3,)),
        ],
        project,
        4 * size,
        args=[
            pltpu.with_memory_space_constraint(a, pltpu.HBM)
            for a in (pair_state, input_weights, input_gains)
        ],
        in_specs=[pl.BlockSpec(memory_space=pltpu.HBM)] * 3,
    )
    mixed, state, gate, wt, gt, ot, iwide, hwide = call(
        mix_first_kernel,
        (
            packed,
            transposed,
            shape((rows, cp, tokens), F32),
            shape((4 * ch, cp), BF16),
            shape((cp, cp), BF16),
            shape((2, cp, ch), BF16),
            shape((cp, LANES), F32),
            shape((2, ch, LANES), F32),
        ),
        [wide, ((cp, LANES), F32)],
        mixing + 2 * small,
        7 * size,
        args=(
            exchange(sent),
            input_weights,
            gate_weights,
            output_weights,
            input_gains,
            hidden_gains,
        ),
    )
    sent, state = call(
        middle_kernel,
        (shape((peers, 32, LANES), BF16), transposed),
        [pitched, pitched, pitched],
        project + small,
        6 * size,
        args=(exchange(mixed), state, gate, hwide, ot, iwide, wt),
    )
    mixed = call(mix_kernel, packed, [], mixing, 3 * size, args=(exchange(sent),))
    out = call(
        last_kernel,
        shape((positions, cp), BF16),
        [pitched, wide, ((positions, LANES), BF16), pltpu.SemaphoreType.DMA((2,))],
        2 * small,
        3 * size,
        args=(exchange(mixed), state, gt, iwide, hwide, ot),
        out_specs=pl.BlockSpec(memory_space=pltpu.HBM),
    )
    return out.reshape(tokens, rows, cp)


def solution(mesh):
    return jax.shard_map(
        on_device,
        mesh=mesh,
        in_specs=(P(AXES, None, None), P(), P(), P(), P(), P()),
        out_specs=P(None, AXES, None),
        check_vma=False,
    )
```

```python
import jax
import jax.numpy as jnp
from jax import lax
from jax.experimental import pallas as pl
from jax.experimental.pallas import tpu as pltpu
from jax.sharding import PartitionSpec as P

epsilon = 1e-05
AXES = ("dap", "rep")
F32 = jnp.float32
BF16 = jnp.bfloat16
LANES = 128
ROWS = 4
PITCH = 24
VMEM_LIMIT = 24 * 1024 * 1024


def dot_nn(a, b):
    return lax.dot_general(a, b, (((1,), (0,)), ((), ())), preferred_element_type=F32)


def dot_nt(a, b):
    return lax.dot_general(a, b, (((1,), (1,)), ((), ())), preferred_element_type=F32)


def half_sigmoid(x):
    return 0.5 * jnp.tanh(x) + 0.5


def norm_wide(x, gain_ref):
    cen = x - jnp.mean(x, axis=0, keepdims=True)
    var = jnp.mean(cen * cen, axis=0, keepdims=True)
    unit = cen * lax.rsqrt(var + epsilon)
    return jnp.concatenate(
        [
            (unit[:, c : c + LANES] * gain_ref[...]).astype(BF16)
            for c in range(0, x.shape[1], LANES)
        ],
        axis=1,
    )


def store_operands(pt, index, rows, left_s, right_s):
    ch = pt.shape[0] // 4
    chunks = pt.shape[1] // LANES
    left = half_sigmoid(pt[ch : 2 * ch]) * pt[:ch]
    right = half_sigmoid(pt[3 * ch :]) * pt[2 * ch : 3 * ch]
    for c in range(chunks):
        sl = pl.ds(c * rows + index, ch, stride=PITCH)
        left_s[sl, :] = left[:, c * LANES : (c + 1) * LANES]
        right_s[sl, :] = right[:, c * LANES : (c + 1) * LANES]


def round_out(parts, out_ref):
    for part, ref in enumerate(parts):
        block = ref[...].reshape(out_ref.shape[0], PITCH, LANES)[:, :16, :]
        out_ref[:, 16 * part : 16 * (part + 1), :] = block.astype(BF16)


def flip(block, factor=1.0):
    return (block.astype(F32).T * factor).astype(BF16)


def flip_projections(w_ref, update, wt_ref):
    ch = w_ref.shape[2] // 4
    for part in range(4):
        block = w_ref[update, :, part * ch : (part + 1) * ch]
        wt_ref[part * ch : (part + 1) * ch, :] = flip(block, 0.5 if part % 2 else 1.0)


def widen(gain):
    return jnp.broadcast_to(gain, (LANES, gain.shape[1])).T


def prepare_kernel(x_hbm, w_hbm, gain_hbm, out_ref, x_ref, w_ref, gain_ref, wt_s, wide_s, left_s, right_s, sem):
    rows, tokens, _ = x_ref.shape
    peers = out_ref.shape[0]
    cols = tokens // peers
    copies = [
        pltpu.make_async_copy(w_hbm.at[0:1], w_ref, sem.at[0]),
        pltpu.make_async_copy(x_hbm, x_ref, sem.at[1]),
        pltpu.make_async_copy(gain_hbm, gain_ref, sem.at[2]),
    ]
    for copy in copies:
        copy.start()
    for copy in copies:
        copy.wait()
    flip_projections(w_ref, 0, wt_s)
    wide_s[...] = widen(gain_ref[0:1, :])
    normed = [norm_wide(x_ref[i].T.astype(F32), wide_s) for i in range(rows)]
    state = [x_ref[i].astype(F32).reshape(peers, cols, LANES) for i in range(rows)]
    out_ref[:, 32:48, :] = jnp.concatenate(state, axis=1).astype(BF16)
    for i in range(rows):
        store_operands(dot_nn(wt_s[...], normed[i]), i, rows, left_s, right_s)
    round_out((left_s, right_s), out_ref)


def gathered(in_ref, part, rows):
    peers = in_ref.shape[0]
    block = in_ref[:, 16 * part : 16 * (part + 1), :].astype(F32)
    return jnp.concatenate(
        [
            block[:, r : r + rows, :].reshape(peers * rows, LANES).astype(BF16)
            for r in range(0, 16, rows)
        ],
        axis=1,
    )


def mix_kernel(in_ref, out_ref):
    peers = in_ref.shape[0]
    rows = ROWS
    mixed = dot_nt(gathered(in_ref, 1, rows), gathered(in_ref, 0, rows))
    blocks = [
        mixed[:, c * LANES : (c + 1) * LANES].reshape(peers, rows, LANES) for c in range(16 // rows)
    ]
    out_ref[...] = jnp.concatenate(blocks, axis=1).astype(BF16)


def mix_first_kernel(
    in_ref,
    w_ref,
    g_ref,
    o_ref,
    igain_ref,
    hgain_ref,
    out_ref,
    state_ref,
    gate_ref,
    wt_ref,
    gt_ref,
    ot_ref,
    iwide_ref,
    hwide_ref,
    wide,
    first_s,
):
    peers = in_ref.shape[0]
    cols, _, tokens = state_ref.shape
    wide[...] = in_ref[:, 32:48, :].astype(F32).reshape(peers * 16, LANES)
    mix_kernel(in_ref, out_ref)
    first = flip(g_ref[0], 0.5)
    first_s[...] = widen(igain_ref[0:1, :])
    normed = []
    for j in range(cols):
        state = wide[pl.ds(j, tokens, stride=cols), :].astype(BF16).T
        state_ref[j] = state
        normed.append(norm_wide(state.astype(F32), first_s))
    for j in range(cols):
        gate_ref[j] = half_sigmoid(dot_nn(first, normed[j]))
    flip_projections(w_ref, 1, wt_ref)
    gt_ref[...] = flip(g_ref[1], 0.5)
    iwide_ref[...] = widen(igain_ref[1:2, :])
    for update in range(2):
        ot_ref[update] = flip(o_ref[update])
        hwide_ref[update] = widen(hgain_ref[update : update + 1, :])


def normalize_mixed(mixed_ref, wide):
    y = mixed_ref[...].astype(F32)
    cen = y - jnp.mean(y, axis=0, keepdims=True)
    var = jnp.mean(cen * cen, axis=0, keepdims=True)
    unit = cen * lax.rsqrt(var + epsilon)
    for h in range(unit.shape[0]):
        wide[PITCH * h : PITCH * h + 16, :] = unit[h]


def hidden_of(wide, j, cols, chunks, gain):
    return jnp.concatenate(
        [
            (wide[pl.ds(c * cols + j, gain.shape[0], stride=PITCH), :] * gain).astype(BF16)
            for c in chunks
        ],
        axis=1,
    )


def middle_kernel(
    mixed_ref, state_ref, gate_ref, hgain_ref, ot_ref, igain_ref, wt_ref, gt_ref, out_ref, next_ref, next_gate_ref, wide, left_s, right_s
):
    cols, _, tokens = state_ref.shape
    chunks = range(tokens // LANES)
    normalize_mixed(mixed_ref, wide)
    normed = []
    for j in range(cols):
        update = dot_nn(ot_ref[0], hidden_of(wide, j, cols, chunks, hgain_ref[0]))
        state = (state_ref[j].astype(F32) + gate_ref[j] * update).astype(BF16)
        next_ref[j] = state
        normed.append(norm_wide(state.astype(F32), igain_ref))
    for j in range(cols):
        store_operands(dot_nn(wt_ref[...], normed[j]), j, cols, left_s, right_s)
        next_gate_ref[j] = half_sigmoid(dot_nn(gt_ref[...], normed[j]))
    round_out((left_s, right_s), out_ref)


def last_kernel(mixed_ref, state_ref, gate_ref, hgain_ref, ot_ref, out_hbm, wide, out_s, out_b, sem):
    cols, _, tokens = state_ref.shape
    parts = sem.shape[0]
    size = tokens // parts
    chunks = size // LANES
    normalize_mixed(mixed_ref, wide)
    copies = []
    for p in range(parts):
        for j in range(cols):
            lanes = slice(p * size, (p + 1) * size)
            hidden = hidden_of(wide, j, cols, range(p * chunks, (p + 1) * chunks), hgain_ref[1])
            update = dot_nn(ot_ref[1], hidden)
            state = (state_ref[j, :, lanes].astype(F32) + gate_ref[j, :, lanes] * update).astype(BF16)
            out_s[pl.ds(p * size * cols + j, size, stride=cols), :] = state.T.astype(F32)
        block = slice(p * size * cols, (p + 1) * size * cols)
        out_b[block, :] = out_s[block, :].astype(BF16)
        copies.append(pltpu.make_async_copy(out_b.at[block], out_hbm.at[block], sem.at[p]))
        copies[-1].start()
    for copy in copies:
        copy.wait()


def call(kernel, out_shape, scratch, flops, moved, args, limit=VMEM_LIMIT, **options):
    return pl.pallas_call(
        kernel,
        out_shape=out_shape,
        scratch_shapes=[pltpu.VMEM(*spec) if isinstance(spec, tuple) else spec for spec in scratch],
        compiler_params=pltpu.CompilerParams(vmem_limit_bytes=limit),
        cost_estimate=pl.CostEstimate(flops=flops, bytes_accessed=moved, transcendentals=0),
        name=kernel.__name__,
        **options,
    )(*args)


def exchange(buffer):
    return lax.all_to_all(buffer, AXES, split_axis=0, concat_axis=0, tiled=True)


def on_device(pair_state, input_weights, gate_weights, output_weights, input_gains, hidden_gains):
    rows, tokens, cp = pair_state.shape
    ch = output_weights.shape[1]
    peers = tokens // rows
    shape = jax.ShapeDtypeStruct
    positions = rows * tokens
    wide = ((positions, LANES), F32)
    pitched = ((peers * PITCH, LANES), F32)
    size = positions * ch * 2
    project = 2 * positions * cp * 4 * ch
    small = 2 * positions * cp * ch
    mixing = 2 * tokens**3
    packed = shape((peers, 16, LANES), BF16)
    transposed = shape((rows, cp, tokens), BF16)
    gating = shape((rows, cp, tokens), F32)

    sent = call(
        prepare_kernel,
        shape((peers, 48, LANES), BF16),
        [
            ((rows, tokens, cp), BF16),
            ((1, cp, 4 * ch), BF16),
            ((2, cp), F32),
            ((4 * ch, cp), BF16),
            ((cp, LANES), F32),
            pitched,
            pitched,
            pltpu.SemaphoreType.DMA((3,)),
        ],
        project,
        4 * size,
        args=[
            pltpu.with_memory_space_constraint(a, pltpu.HBM)
            for a in (pair_state, input_weights, input_gains)
        ],
        in_specs=[pl.BlockSpec(memory_space=pltpu.HBM)] * 3,
    )
    mixed, state, gate, wt, gt, ot, iwide, hwide = call(
        mix_first_kernel,
        (
            packed,
            transposed,
            gating,
            shape((4 * ch, cp), BF16),
            shape((cp, cp), BF16),
            shape((2, cp, ch), BF16),
            shape((cp, LANES), F32),
            shape((2, ch, LANES), F32),
        ),
        [wide, ((cp, LANES), F32)],
        mixing + 2 * small,
        7 * size,
        args=(
            exchange(sent),
            input_weights,
            gate_weights,
            output_weights,
            input_gains,
            hidden_gains,
        ),
    )
    sent, state, gate = call(
        middle_kernel,
        (shape((peers, 32, LANES), BF16), transposed, gating),
        [pitched, pitched, pitched],
        project + 2 * small,
        8 * size,
        args=(exchange(mixed), state, gate, hwide, ot, iwide, wt, gt),
    )
    mixed = call(mix_kernel, packed, [], mixing, 3 * size, args=(exchange(sent),))
    out = call(
        last_kernel,
        shape((positions, cp), BF16),
        [pitched, wide, ((positions, LANES), BF16), pltpu.SemaphoreType.DMA((2,))],
        small,
        5 * size,
        args=(exchange(mixed), state, gate, hwide, ot),
        out_specs=pl.BlockSpec(memory_space=pltpu.HBM),
    )
    return out.reshape(tokens, rows, cp)


def solution(mesh):
    return jax.shard_map(
        on_device,
        mesh=mesh,
        in_specs=(P(AXES, None, None), P(), P(), P(), P(), P()),
        out_specs=P(None, AXES, None),
        check_vma=False,
    )
```

```python
import jax
import jax.numpy as jnp
from jax import lax
from jax.experimental import pallas as pl
from jax.experimental.pallas import tpu as pltpu
from jax.sharding import PartitionSpec as P

epsilon = 1e-05
AXES = ("dap", "rep")
F32 = jnp.float32
BF16 = jnp.bfloat16
LANES = 128
ROWS = 4
PITCH = 24
VMEM_LIMIT = 24 * 1024 * 1024


def dot_nn(a, b):
    return lax.dot_general(a, b, (((1,), (0,)), ((), ())), preferred_element_type=F32)


def dot_nt(a, b):
    return lax.dot_general(a, b, (((1,), (1,)), ((), ())), preferred_element_type=F32)


def half_sigmoid(x):
    return 0.5 * jnp.tanh(x) + 0.5


def norm_wide(x, gain_ref):
    cen = x - jnp.mean(x, axis=0, keepdims=True)
    var = jnp.mean(cen * cen, axis=0, keepdims=True)
    unit = cen * lax.rsqrt(var + epsilon)
    return jnp.concatenate(
        [
            (unit[:, c : c + LANES] * gain_ref[...]).astype(BF16)
            for c in range(0, x.shape[1], LANES)
        ],
        axis=1,
    )


def store_operands(pt, index, rows, left_s, right_s):
    ch = pt.shape[0] // 4
    chunks = pt.shape[1] // LANES
    left = half_sigmoid(pt[ch : 2 * ch]) * pt[:ch]
    right = half_sigmoid(pt[3 * ch :]) * pt[2 * ch : 3 * ch]
    for c in range(chunks):
        sl = pl.ds(c * rows + index, ch, stride=PITCH)
        left_s[sl, :] = left[:, c * LANES : (c + 1) * LANES]
        right_s[sl, :] = right[:, c * LANES : (c + 1) * LANES]


def round_out(parts, out_ref):
    for part, ref in enumerate(parts):
        block = ref[...].reshape(out_ref.shape[0], PITCH, LANES)[:, :16, :]
        out_ref[:, 16 * part : 16 * (part + 1), :] = block.astype(BF16)


def flip(block, factor=1.0):
    return (block.astype(F32).T * factor).astype(BF16)


def flip_projections(w_ref, update, wt_ref):
    ch = w_ref.shape[2] // 4
    for part in range(4):
        block = w_ref[update, :, part * ch : (part + 1) * ch]
        wt_ref[part * ch : (part + 1) * ch, :] = flip(block, 0.5 if part % 2 else 1.0)


def widen(gain):
    return jnp.broadcast_to(gain, (LANES, gain.shape[1])).T


def prepare_kernel(x_hbm, w_hbm, gain_hbm, out_ref, x_ref, w_ref, gain_ref, wt_s, wide_s, left_s, right_s, sem):
    rows, tokens, _ = x_ref.shape
    peers = out_ref.shape[0]
    cols = tokens // peers
    copies = [
        pltpu.make_async_copy(gain_hbm, gain_ref, sem.at[2]),
        pltpu.make_async_copy(w_hbm.at[0:1], w_ref, sem.at[0]),
        pltpu.make_async_copy(x_hbm, x_ref, sem.at[1]),
    ]
    for copy in copies:
        copy.start()
    copies[0].wait()
    wide_s[...] = widen(gain_ref[0:1, :])
    copies[1].wait()
    flip_projections(w_ref, 0, wt_s)
    copies[2].wait()
    normed = [norm_wide(x_ref[i].T.astype(F32), wide_s) for i in range(rows)]
    state = [x_ref[i].astype(F32).reshape(peers, cols, LANES) for i in range(rows)]
    out_ref[:, 32:48, :] = jnp.concatenate(state, axis=1).astype(BF16)
    for i in range(rows):
        store_operands(dot_nn(wt_s[...], normed[i]), i, rows, left_s, right_s)
    round_out((left_s, right_s), out_ref)


def gathered(in_ref, part, rows):
    peers = in_ref.shape[0]
    block = in_ref[:, 16 * part : 16 * (part + 1), :].astype(F32)
    return jnp.concatenate(
        [
            block[:, r : r + rows, :].reshape(peers * rows, LANES).astype(BF16)
            for r in range(0, 16, rows)
        ],
        axis=1,
    )


def mix_kernel(in_ref, out_ref):
    peers = in_ref.shape[0]
    rows = ROWS
    mixed = dot_nt(gathered(in_ref, 1, rows), gathered(in_ref, 0, rows))
    blocks = [
        mixed[:, c * LANES : (c + 1) * LANES].reshape(peers, rows, LANES) for c in range(16 // rows)
    ]
    out_ref[...] = jnp.concatenate(blocks, axis=1).astype(BF16)


def mix_first_kernel(
    in_ref,
    w_ref,
    g_ref,
    o_ref,
    igain_ref,
    hgain_ref,
    out_ref,
    state_ref,
    wt_ref,
    gt_ref,
    ot_ref,
    iwide_ref,
    hwide_ref,
    wide,
):
    peers = in_ref.shape[0]
    cols, _, tokens = state_ref.shape
    wide[...] = in_ref[:, 32:48, :].astype(F32).reshape(peers * 16, LANES)
    mix_kernel(in_ref, out_ref)
    for j in range(cols):
        state_ref[j] = wide[pl.ds(j, tokens, stride=cols), :].astype(BF16).T
    flip_projections(w_ref, 1, wt_ref)
    for update in range(2):
        gt_ref[update] = flip(g_ref[update], 0.5)
        iwide_ref[update] = widen(igain_ref[update : update + 1, :])
        ot_ref[update] = flip(o_ref[update])
        hwide_ref[update] = widen(hgain_ref[update : update + 1, :])


def normalize_mixed(mixed_ref, wide):
    y = mixed_ref[...].astype(F32)
    cen = y - jnp.mean(y, axis=0, keepdims=True)
    var = jnp.mean(cen * cen, axis=0, keepdims=True)
    unit = cen * lax.rsqrt(var + epsilon)
    for h in range(unit.shape[0]):
        wide[PITCH * h : PITCH * h + 16, :] = unit[h]


def hidden_of(wide, j, cols, chunks, gain):
    return jnp.concatenate(
        [
            (wide[pl.ds(c * cols + j, gain.shape[0], stride=PITCH), :] * gain).astype(BF16)
            for c in chunks
        ],
        axis=1,
    )


def middle_kernel(
    mixed_ref, state_ref, hgain_ref, ot_ref, igain_ref, wt_ref, gt_ref, out_ref, next_ref, next_gate_ref, wide, left_s, right_s
):
    cols, _, tokens = state_ref.shape
    chunks = range(tokens // LANES)
    normalize_mixed(mixed_ref, wide)
    normed = []
    for j in range(cols):
        update = dot_nn(ot_ref[0], hidden_of(wide, j, cols, chunks, hgain_ref[0]))
        old = state_ref[j].astype(F32)
        gate = half_sigmoid(dot_nn(gt_ref[0], norm_wide(old, igain_ref.at[0])))
        state = (old + gate * update).astype(BF16)
        next_ref[j] = state
        normed.append(norm_wide(state.astype(F32), igain_ref.at[1]))
    for j in range(cols):
        store_operands(dot_nn(wt_ref[...], normed[j]), j, cols, left_s, right_s)
        next_gate_ref[j] = half_sigmoid(dot_nn(gt_ref[1], normed[j]))
    round_out((left_s, right_s), out_ref)


def last_kernel(mixed_ref, state_ref, gate_ref, hgain_ref, ot_ref, out_hbm, wide, out_s, out_b, sem):
    cols, _, tokens = state_ref.shape
    parts = sem.shape[0]
    size = tokens // parts
    chunks = size // LANES
    normalize_mixed(mixed_ref, wide)
    copies = []
    for p in range(parts):
        for j in range(cols):
            lanes = slice(p * size, (p + 1) * size)
            hidden = hidden_of(wide, j, cols, range(p * chunks, (p + 1) * chunks), hgain_ref[1])
            update = dot_nn(ot_ref[1], hidden)
            state = (state_ref[j, :, lanes].astype(F32) + gate_ref[j, :, lanes] * update).astype(BF16)
            out_s[pl.ds(p * size * cols + j, size, stride=cols), :] = state.T.astype(F32)
        block = slice(p * size * cols, (p + 1) * size * cols)
        out_b[block, :] = out_s[block, :].astype(BF16)
        copies.append(pltpu.make_async_copy(out_b.at[block], out_hbm.at[block], sem.at[p]))
        copies[-1].start()
    for copy in copies:
        copy.wait()


def call(kernel, out_shape, scratch, flops, moved, args, limit=VMEM_LIMIT, **options):
    return pl.pallas_call(
        kernel,
        out_shape=out_shape,
        scratch_shapes=[pltpu.VMEM(*spec) if isinstance(spec, tuple) else spec for spec in scratch],
        compiler_params=pltpu.CompilerParams(vmem_limit_bytes=limit),
        cost_estimate=pl.CostEstimate(flops=flops, bytes_accessed=moved, transcendentals=0),
        name=kernel.__name__,
        **options,
    )(*args)


def exchange(buffer):
    return lax.all_to_all(buffer, AXES, split_axis=0, concat_axis=0, tiled=True)


def on_device(pair_state, input_weights, gate_weights, output_weights, input_gains, hidden_gains):
    rows, tokens, cp = pair_state.shape
    ch = output_weights.shape[1]
    peers = tokens // rows
    shape = jax.ShapeDtypeStruct
    positions = rows * tokens
    wide = ((positions, LANES), F32)
    pitched = ((peers * PITCH, LANES), F32)
    size = positions * ch * 2
    project = 2 * positions * cp * 4 * ch
    small = 2 * positions * cp * ch
    mixing = 2 * tokens**3
    packed = shape((peers, 16, LANES), BF16)
    transposed = shape((rows, cp, tokens), BF16)
    gating = shape((rows, cp, tokens), F32)

    sent = call(
        prepare_kernel,
        shape((peers, 48, LANES), BF16),
        [
            ((rows, tokens, cp), BF16),
            ((1, cp, 4 * ch), BF16),
            ((2, cp), F32),
            ((4 * ch, cp), BF16),
            ((cp, LANES), F32),
            pitched,
            pitched,
            pltpu.SemaphoreType.DMA((3,)),
        ],
        project,
        4 * size,
        args=[
            pltpu.with_memory_space_constraint(a, pltpu.HBM)
            for a in (pair_state, input_weights, input_gains)
        ],
        in_specs=[pl.BlockSpec(memory_space=pltpu.HBM)] * 3,
    )
    mixed, state, wt, gt, ot, iwide, hwide = call(
        mix_first_kernel,
        (
            packed,
            transposed,
            shape((4 * ch, cp), BF16),
            shape((2, cp, cp), BF16),
            shape((2, cp, ch), BF16),
            shape((2, cp, LANES), F32),
            shape((2, ch, LANES), F32),
        ),
        [wide],
        mixing,
        5 * size,
        args=(
            exchange(sent),
            input_weights,
            gate_weights,
            output_weights,
            input_gains,
            hidden_gains,
        ),
    )
    sent, state, gate = call(
        middle_kernel,
        (shape((peers, 32, LANES), BF16), transposed, gating),
        [pitched, pitched, pitched],
        project + 3 * small,
        8 * size,
        args=(exchange(mixed), state, hwide, ot, iwide, wt, gt),
    )
    mixed = call(mix_kernel, packed, [], mixing, 3 * size, args=(exchange(sent),))
    out = call(
        last_kernel,
        shape((positions, cp), BF16),
        [pitched, wide, ((positions, LANES), BF16), pltpu.SemaphoreType.DMA((4,))],
        small,
        5 * size,
        args=(exchange(mixed), state, gate, hwide, ot),
        out_specs=pl.BlockSpec(memory_space=pltpu.HBM),
    )
    return out.reshape(tokens, rows, cp)


def solution(mesh):
    return jax.shard_map(
        on_device,
        mesh=mesh,
        in_specs=(P(AXES, None, None), P(), P(), P(), P(), P()),
        out_specs=P(None, AXES, None),
        check_vma=False,
    )
```
